32 devices in a mesh: grp: 2 (over y), blk: 16 (over z, x, core).
Axes of the slice: x: 2, y: 2, z: 4, core: 2. Of those that a mesh axis runs over, the one named last changes fastest.
Arguments:
- couplings: bfloat16 [64, 2, 32, 30720], P('blk', None, 'grp'), parts along dimension 2, may hold values from -2 to 2
- elec_vectors: int32 [3, 64], P(None, 'blk'), may hold values from -8 to 8
- phon_vectors: int32 [3, 32], P(None, 'grp'), parts along dimension 1, may hold values from -4 to 4
- degeneracy: int32 [32], P('grp'), parts along dimension 0, may hold values from 1 to 8
- k_point: float32 [6], P('grp'), parts along dimension 0, may hold values from 0 to 1
- q_index: int32 [3, 512], P(None, 'blk'), may hold values from 0 to 15
Outputs:
- bloch_coupling: bfloat16 [2, 1024, 30720], P(None, ('grp', 'blk')), parts along dimension 1
The draws below stay inside these ranges and needn't reach their ends.
There are 2 independent parts, one for each index of `grp`. The reference program is written for one: setup_inputs(seed, part) draws one part's arguments, and reference() takes and returns one part's arrays. A program takes and returns all parts, laid end to end along the dimension named above; an argument that names none is the same for every part. Nothing has to cross between parts.
All inputs are finite; a program needn't handle non-finite values.
Results may differ from the reference program's by a relative error of at most 0.0059.
Values may be sent and summed in bfloat16 or wider, within the bound.
No kernel may reach another device: no remote copies, remote signals or barrier semaphores. Data moves between devices by JAX's collectives and lax.ppermute only.
A program may use at most 64 MiB of HBM per device.

```python
import math
import jax
import jax.numpy as jnp

RP = 16
RE_DEV = 4
NG = 16
W = 30720
RE = 64
QPTS = 512
N_BLK = 16


def place_ends(array, own_key, smallest, largest):
    place = [jax.random.randint(jax.random.fold_in(own_key, axis), (), 0, length) for axis, length in enumerate(array.shape)]
    longest = array.shape.index(max(array.shape))
    next_to = place[:longest] + [(place[longest] + 1) % array.shape[longest]] + place[longest + 1:]
    return array.at[tuple(place)].set(smallest).at[tuple(next_to)].set(largest)


def block_scale(rng, extent, pieces, low, top_value):
    factor_of = 1.0
    for dim, blocks in pieces:
        draws = jax.random.uniform(jax.random.fold_in(jax.random.fold_in(rng, 6), dim), (blocks,), jnp.float32, low / len(pieces), top_value / len(pieces))
        factor_of = factor_of * jnp.repeat(jnp.exp(draws), extent[dim] // blocks).reshape((-1,) + (1,) * (len(extent) - 1 - dim))
    return factor_of


def bell_draw(rng, extent, deviation, reach, pieces=(), dtype=jnp.bfloat16):
    array = deviation * jax.random.normal(rng, extent, jnp.float32)
    if pieces:
        array = array * block_scale(rng, extent, pieces, -0.22, 0.18)
    return jnp.clip(array, -reach, reach).astype(dtype)


def setup_inputs(seed: int = 0, part: int = 0) -> dict:
    keys = jax.random.split(jax.random.key(seed), 7)
    part_keys = jax.random.split(jax.random.fold_in(keys[6], part), 7)
    couplings = bell_draw(part_keys[0], (RE, 2, RP, W), ((RE_DEV * N_BLK) ** -0.5), 2.0, ((0, 16),))
    elec_vectors = place_ends(jax.random.randint(keys[1], (3, RE), -8, 9), jax.random.fold_in(keys[1], 1), -8, 8).astype(jnp.int32)
    phon_vectors = place_ends(jax.random.randint(part_keys[2], (3, RP), -4, 5), jax.random.fold_in(part_keys[2], 1), -4, 4).astype(jnp.int32)
    degeneracy = place_ends(jax.random.randint(part_keys[3], (RP,), 1, 9), jax.random.fold_in(part_keys[3], 1), 1, 8).astype(jnp.int32)
    k_point = jnp.clip(jax.random.uniform(part_keys[4], (3,), jnp.float32, 0.0, 1.0), 0.0, 1.0)
    q_index = place_ends(jax.random.randint(keys[5], (3, QPTS), 0, NG), jax.random.fold_in(keys[5], 1), 0, NG - 1).astype(jnp.int32)
    return dict(couplings=couplings, elec_vectors=elec_vectors, phon_vectors=phon_vectors, degeneracy=degeneracy, k_point=k_point, q_index=q_index)


def k_phases(k_point, elec_vectors):
    theta = 2.0 * math.pi * jnp.sum(k_point[:, None] * elec_vectors.astype(jnp.float32), axis=0)
    return jnp.cos(theta).astype(jnp.bfloat16), jnp.sin(theta).astype(jnp.bfloat16)


def k_matrix(k_point, elec_vectors):
    kcos, ksin = k_phases(k_point, elec_vectors)
    upper = jnp.stack([kcos, -ksin], axis=1).reshape(-1)
    lower = jnp.stack([ksin, kcos], axis=1).reshape(-1)
    return jnp.stack([upper, lower], axis=0)


def q_matrix(q_index, phon_vectors, degeneracy):
    dots = jnp.sum(q_index[:, :, None] * phon_vectors[:, None, :], axis=0)
    wound = jnp.mod(dots, NG).astype(jnp.float32)
    angle = 2.0 * math.pi * wound / NG
    weight = 1.0 / degeneracy.astype(jnp.float32)
    qcos = jnp.cos(angle) * weight[None, :]
    qsin = jnp.sin(angle) * weight[None, :]
    top = jnp.concatenate([qcos, -qsin], axis=1)
    bottom = jnp.concatenate([qsin, qcos], axis=1)
    return jnp.concatenate([top, bottom], axis=0).astype(jnp.bfloat16)


def reference(couplings, elec_vectors, phon_vectors, degeneracy, k_point, q_index):
    kmat = k_matrix(k_point, elec_vectors)
    flat = couplings.reshape(RE * 2, RP * W)
    summed = jnp.dot(kmat, flat, preferred_element_type=jnp.float32).astype(jnp.bfloat16)
    qmat = q_matrix(q_index, phon_vectors, degeneracy)
    result = jnp.dot(qmat, summed.reshape(2 * RP, W), preferred_element_type=jnp.float32)
    return result.astype(jnp.bfloat16).reshape(2, QPTS, W)
```

```python
import math

import jax
import jax.numpy as jnp
from jax import lax
from jax.experimental import pallas as pl
from jax.experimental.pallas import tpu as pltpu
from jax.sharding import PartitionSpec as P

NG = 16
BLOCKS = 8
HALF = 4


def block_of(me, position):
    core = me % 2
    first, second = (me // 2) % 2, (me // 4) % 2
    flip = 7 - position
    owner = (core + flip // 4) % 2
    high = jnp.where(owner == 0, first, second)
    low = jnp.where(owner == 0, second, first)
    high = (high + (flip // 2) % 2) % 2
    low = (low + flip % 2) % 2
    return owner * 4 + high * 2 + low


def partial_kernel(me_ref, k_ref, elec_ref, couplings_ref, out_ref, kmat):
    re_here = couplings_ref.shape[0]
    slab = couplings_ref.shape[2]
    rows, depth = kmat.shape

    @pl.when(pl.program_id(0) == 0)
    def _():
        row = lax.broadcasted_iota(jnp.int32, (rows, depth), 0)
        col = lax.broadcasted_iota(jnp.int32, (rows, depth), 1)
        vector = col // (2 * slab)
        theta = jnp.zeros((rows, depth), jnp.float32)
        for e in range(re_here):
            total = k_ref[0] * elec_ref[0, e].astype(jnp.float32)
            total += k_ref[1] * elec_ref[1, e].astype(jnp.float32)
            total += k_ref[2] * elec_ref[2, e].astype(jnp.float32)
            theta = jnp.where(vector == e, 2.0 * math.pi * total, theta)
        cos, sin = jnp.cos(theta), jnp.sin(theta)
        out_part, in_part = row // slab, (col // slab) % 2
        value = jnp.where(out_part == in_part, cos, jnp.where(out_part == 1, sin, -sin))
        kmat[...] = jnp.where(row % slab == col % slab, value, 0.0).astype(kmat.dtype)

    table = couplings_ref[...].reshape(depth, couplings_ref.shape[3])
    out_ref[0] = jnp.dot(kmat[...], table, preferred_element_type=jnp.float32).astype(out_ref.dtype)


def partial_sums(me, k_point, elec_vectors, couplings, offset, dtype):
    re_here, parts, slab, width = couplings.shape
    columns = width // BLOCKS
    return pl.pallas_call(
        partial_kernel,
        grid_spec=pltpu.PrefetchScalarGridSpec(
            num_scalar_prefetch=3,
            grid=(HALF,),
            in_specs=[
                pl.BlockSpec(
                    (re_here, parts, slab, columns),
                    lambda j, me_ref, *_: (0, 0, 0, block_of(me_ref[0], j + offset)),
                )
            ],
            out_specs=pl.BlockSpec((1, parts * slab, columns), lambda j, *_: (j, 0, 0)),
            scratch_shapes=[pltpu.VMEM((parts * slab, re_here * parts * slab), jnp.bfloat16)],
        ),
        out_shape=jax.ShapeDtypeStruct((HALF, parts * slab, columns), dtype),
        compiler_params=pltpu.CompilerParams(vmem_limit_bytes=24 * 2**20),
        cost_estimate=pl.CostEstimate(
            flops=2 * (parts * slab) ** 2 * re_here * width // 2, bytes_accessed=couplings.size, transcendentals=0
        ),
    )(me, k_point, elec_vectors, couplings)


def q_matrix(q_index, phon_vectors, degeneracy):
    dots = jnp.sum(q_index[:, :, None] * phon_vectors[:, None, :], axis=0)
    wound = jnp.mod(dots, NG).astype(jnp.float32)
    angle = 2.0 * math.pi * wound / NG
    weight = 1.0 / degeneracy.astype(jnp.float32)
    qcos = jnp.cos(angle) * weight[None, :]
    qsin = jnp.sin(angle) * weight[None, :]
    top = jnp.concatenate([qcos, -qsin], axis=1)
    bottom = jnp.concatenate([qsin, qcos], axis=1)
    return jnp.concatenate([top, bottom], axis=0).astype(jnp.bfloat16)


def bloch_kernel(me_ref, qmat_ref, *refs):
    slab_ref, out_ref = refs[0], refs[-1]
    points = out_ref.shape[1]
    result = jnp.dot(qmat_ref[...], slab_ref[0], preferred_element_type=jnp.float32).astype(out_ref.dtype)
    out_ref[0] = result[:points]
    out_ref[1] = result[points:]


def bloch(me, qmat, slab, offset, width, out=None):
    blocks, rows, columns = slab.shape
    points = qmat.shape[0] // 2
    in_specs = [
        pl.BlockSpec(qmat.shape, lambda j, *_: (0, 0)),
        pl.BlockSpec((1, rows, columns), lambda j, *_: (j, 0, 0)),
    ]
    operands = [me, qmat, slab]
    aliases = {}
    if out is not None:
        in_specs.append(pl.BlockSpec(memory_space=pl.ANY))
        operands.append(out)
        aliases = {3: 0}
    return pl.pallas_call(
        bloch_kernel,
        grid_spec=pltpu.PrefetchScalarGridSpec(
            num_scalar_prefetch=1,
            grid=(blocks,),
            in_specs=in_specs,
            out_specs=pl.BlockSpec(
                (2, points, columns), lambda j, me_ref, *_: (0, 0, block_of(me_ref[0], j + offset))
            ),
        ),
        out_shape=jax.ShapeDtypeStruct((2, points, width), jnp.bfloat16),
        input_output_aliases=aliases,
        compiler_params=pltpu.CompilerParams(vmem_limit_bytes=24 * 2**20),
        cost_estimate=pl.CostEstimate(
            flops=4 * points * rows * blocks * columns,
            bytes_accessed=4 * points * blocks * columns,
            transcendentals=0,
        ),
    )(*operands)


def on_device(devices, couplings, elec_vectors, phon_vectors, degeneracy, k_point, q_index):
    width = couplings.shape[3]
    wire = jnp.bfloat16
    me = lax.axis_index("blk").astype(jnp.int32).reshape(1)

    def send(array, even, odd):
        return lax.ppermute(array, "blk", [(i, i ^ (odd if i % 2 else even)) for i in range(devices)])

    theirs = partial_sums(me, k_point, elec_vectors, couplings, 0, wire)
    got = send(theirs, 1, 1)
    own = partial_sums(me, k_point, elec_vectors, couplings, HALF, jnp.float32)
    qmat = q_matrix(q_index, phon_vectors, degeneracy)

    first = send((own[:2] + got[:2].astype(jnp.float32)).astype(wire), 2, 4)
    own = own[2:] + got[2:].astype(jnp.float32)
    second = send((own[:1] + first[:1].astype(jnp.float32)).astype(wire), 4, 2)
    own = own[1:] + first[1:].astype(jnp.float32) + second.astype(jnp.float32)
    step = 8
    while step < devices:
        own = own + send(own.astype(wire), step, step).astype(jnp.float32)
        step *= 2
    block = own.astype(wire)
    pair = jnp.concatenate([send(block, 4, 2), block])
    quad = jnp.concatenate([send(pair, 2, 4), pair])
    rest = send(quad, 1, 1)
    out = bloch(me, qmat, quad, HALF, width)
    return bloch(me, qmat, rest, 0, width, out)


def solution(mesh):
    placed = (
        P("blk", None, "grp", None),
        P(None, "blk"),
        P(None, "grp"),
        P("grp"),
        P("grp"),
        P(None, "blk"),
    )
    devices = mesh.shape["blk"]
    return jax.shard_map(
        lambda *arrays: on_device(devices, *arrays),
        mesh=mesh,
        in_specs=placed,
        out_specs=P(None, ("grp", "blk"), None),
        check_vma=False,
    )
```

```python
import math

import jax
import jax.numpy as jnp
from jax import lax
from jax.experimental import pallas as pl
from jax.experimental.pallas import tpu as pltpu
from jax.sharding import PartitionSpec as P

NG = 16
STREAMS = 1
HALF = 4
BLOCKS = 2 * HALF * STREAMS
VMEM_LIMIT = 24 * 2**20


def block_of(me, position):
    core = me % 2
    first, second = (me // 2) % 2, (me // 4) % 2
    flip = 7 - position
    owner = (core + flip // 4) % 2
    high = jnp.where(owner == 0, first, second)
    low = jnp.where(owner == 0, second, first)
    high = (high + (flip // 2) % 2) % 2
    low = (low + flip % 2) % 2
    return owner * 4 + high * 2 + low


def columns_at(me, position, stream, columns):
    start = (stream * 2 * HALF + block_of(me, position)) * columns
    return pl.ds(pl.multiple_of(start, 128), columns)


def partial_kernel(offset, stream, me_ref, k_hbm, elec_hbm, couplings_hbm, out_ref, k_buf, elec_buf, table, small, sems):
    blocks, rows, columns = out_ref.shape
    re_here, parts, slab = couplings_hbm.shape[:3]
    depth = re_here * parts * slab
    small_copies = [
        pltpu.make_async_copy(k_hbm, k_buf, small.at[0]),
        pltpu.make_async_copy(elec_hbm, elec_buf, small.at[1]),
    ]
    for copy in small_copies:
        copy.start()
    copies = []
    for j in range(blocks):
        place = columns_at(me_ref[0], offset + j, stream, columns)
        copies.append(pltpu.make_async_copy(couplings_hbm.at[:, :, :, place], table.at[j], sems.at[j]))
        copies[-1].start()
    for copy in small_copies:
        copy.wait()

    terms = [k_buf[:, d : d + 1] * elec_buf[d : d + 1, :].astype(jnp.float32) for d in range(3)]
    theta_here = 2.0 * math.pi * (terms[0] + terms[1] + terms[2])
    vector = lax.broadcasted_iota(jnp.int32, (8, depth), 1) // (parts * slab)
    theta = jnp.zeros((8, depth), jnp.float32)
    for e in range(re_here):
        theta = jnp.where(vector == e, theta_here[:, e : e + 1], theta)
    cos = jnp.cos(theta)[:1]
    sin = jnp.sin(theta)[:1]
    row = lax.broadcasted_iota(jnp.int32, (rows, depth), 0)
    col = lax.broadcasted_iota(jnp.int32, (rows, depth), 1)
    out_part, in_part = row // slab, (col // slab) % parts
    value = jnp.where(out_part == in_part, cos, jnp.where(out_part == 1, sin, -sin))
    kmat = jnp.where(row % slab == col % slab, value, 0.0).astype(table.dtype)

    for j in range(blocks):
        copies[j].wait()
        flat = table[j].reshape(depth, columns)
        out_ref[j] = jnp.dot(kmat, flat, preferred_element_type=jnp.float32).astype(out_ref.dtype)


def partial_sums(me, k_point, elec_vectors, couplings, offset, stream, dtype):
    re_here, parts, slab, width = couplings.shape
    columns = width // BLOCKS
    hbm = pl.BlockSpec(memory_space=pltpu.HBM)
    k_row = k_point.reshape(1, 3)
    return pl.pallas_call(
        lambda *refs: partial_kernel(offset, stream, *refs),
        in_specs=[pl.BlockSpec(memory_space=pltpu.SMEM), hbm, hbm, hbm],
        out_specs=pl.BlockSpec(memory_space=pltpu.VMEM),
        out_shape=jax.ShapeDtypeStruct((HALF, parts * slab, columns), dtype),
        scratch_shapes=[
            pltpu.VMEM((1, 3), jnp.float32),
            pltpu.VMEM(elec_vectors.shape, jnp.int32),
            pltpu.VMEM((HALF, re_here, parts, slab, columns), couplings.dtype),
            pltpu.SemaphoreType.DMA((2,)),
            pltpu.SemaphoreType.DMA((HALF,)),
        ],
        compiler_params=pltpu.CompilerParams(vmem_limit_bytes=VMEM_LIMIT),
        cost_estimate=pl.CostEstimate(
            flops=2 * (parts * slab) ** 2 * re_here * HALF * columns,
            bytes_accessed=2 * parts * slab * re_here * HALF * columns,
            transcendentals=0,
        ),
    )(
        me,
        pltpu.with_memory_space_constraint(k_row, pltpu.HBM),
        pltpu.with_memory_space_constraint(elec_vectors, pltpu.HBM),
        pltpu.with_memory_space_constraint(couplings, pltpu.HBM),
    )


def q_matrix(q_index, phon_vectors, degeneracy):
    dots = jnp.sum(q_index[:, :, None] * phon_vectors[:, None, :], axis=0)
    wound = jnp.mod(dots, NG).astype(jnp.float32)
    angle = 2.0 * math.pi * wound / NG
    weight = 1.0 / degeneracy.astype(jnp.float32)
    qcos = jnp.cos(angle) * weight[None, :]
    qsin = jnp.sin(angle) * weight[None, :]
    top = jnp.concatenate([qcos, -qsin], axis=1)
    bottom = jnp.concatenate([qsin, qcos], axis=1)
    return jnp.concatenate([top, bottom], axis=0).astype(jnp.bfloat16)


def bloch_kernel(offset, stream, me_ref, qmat_ref, slab_ref, *refs):
    out_hbm, buffer, sems = refs[-3:]
    blocks, rows, columns = slab_ref.shape
    points = out_hbm.shape[1]
    copies = []
    for j in range(blocks):
        result = jnp.dot(qmat_ref[...], slab_ref[j], preferred_element_type=jnp.float32).astype(buffer.dtype)
        buffer[j, 0] = result[:points]
        buffer[j, 1] = result[points:]
        place = columns_at(me_ref[0], offset + j, stream, columns)
        copies.append(pltpu.make_async_copy(buffer.at[j], out_hbm.at[:, :, place], sems.at[j]))
        copies[-1].start()
    for copy in copies:
        copy.wait()


def bloch(me, qmat, slab, offset, stream, width, out=None):
    blocks, rows, columns = slab.shape
    points = qmat.shape[0] // 2
    vmem, hbm = pl.BlockSpec(memory_space=pltpu.VMEM), pl.BlockSpec(memory_space=pltpu.HBM)
    before = () if out is None else (out,)
    return pl.pallas_call(
        lambda *refs: bloch_kernel(offset, stream, *refs),
        in_specs=[pl.BlockSpec(memory_space=pltpu.SMEM), vmem, vmem] + [hbm] * len(before),
        out_specs=hbm,
        out_shape=jax.ShapeDtypeStruct((2, points, width), jnp.bfloat16),
        scratch_shapes=[
            pltpu.VMEM((blocks, 2, points, columns), jnp.bfloat16),
            pltpu.SemaphoreType.DMA((blocks,)),
        ],
        input_output_aliases={3: 0} if before else {},
        compiler_params=pltpu.CompilerParams(vmem_limit_bytes=VMEM_LIMIT),
        cost_estimate=pl.CostEstimate(
            flops=4 * points * rows * blocks * columns,
            bytes_accessed=4 * points * blocks * columns,
            transcendentals=0,
        ),
    )(me, qmat, slab, *before)


def on_device(devices, couplings, elec_vectors, phon_vectors, degeneracy, k_point, q_index):
    width = couplings.shape[3]
    wire = jnp.bfloat16
    me = lax.axis_index("blk").astype(jnp.int32).reshape(1)

    def send(array, even, odd):
        return lax.ppermute(array, "blk", [(i, i ^ (odd if i % 2 else even)) for i in range(devices)])

    qmat = q_matrix(q_index, phon_vectors, degeneracy)
    out = None
    for stream in range(STREAMS):
        theirs = partial_sums(me, k_point, elec_vectors, couplings, 0, stream, wire)
        got = send(theirs, 1, 1)
        own = partial_sums(me, k_point, elec_vectors, couplings, HALF, stream, jnp.float32)

        first = send((own[:2] + got[:2].astype(jnp.float32)).astype(wire), 2, 4)
        own = own[2:] + got[2:].astype(jnp.float32)
        second = send((own[:1] + first[:1].astype(jnp.float32)).astype(wire), 4, 2)
        own = own[1:] + first[1:].astype(jnp.float32) + second.astype(jnp.float32)
        step = 8
        while step < devices:
            own = own + send(own.astype(wire), step, step).astype(jnp.float32)
            step *= 2
        block = own.astype(wire)
        pair = jnp.concatenate([send(block, 4, 2), block])
        quad = jnp.concatenate([send(pair, 2, 4), pair])
        rest = send(quad, 1, 1)
        out = bloch(me, qmat, quad, HALF, stream, width, out)
        out = bloch(me, qmat, rest, 0, stream, width, out)
    return out


def solution(mesh):
    placed = (
        P("blk", None, "grp", None),
        P(None, "blk"),
        P(None, "grp"),
        P("grp"),
        P("grp"),
        P(None, "blk"),
    )
    devices = mesh.shape["blk"]
    return jax.shard_map(
        lambda *arrays: on_device(devices, *arrays),
        mesh=mesh,
        in_specs=placed,
        out_specs=P(None, ("grp", "blk"), None),
        check_vma=False,
    )
```

```python
import math

import jax
import jax.numpy as jnp
from jax import lax
from jax.experimental import pallas as pl
from jax.experimental.pallas import tpu as pltpu
from jax.sharding import PartitionSpec as P

NG = 16
STREAMS = 2
HALF = 4
BLOCKS = 2 * HALF * STREAMS
VMEM_LIMIT = 24 * 2**20


def block_of(me, position):
    flip = 7 - position
    core = (me % 2 + flip // 4) % 2
    first = ((me // 2) % 2 + (flip // 2) % 2) % 2
    second = ((me // 4) % 2 + flip % 2) % 2
    return core * 4 + first * 2 + second


def columns_at(me, position, stream, columns):
    start = (stream * 2 * HALF + block_of(me, position)) * columns
    return pl.ds(pl.multiple_of(start, 128), columns)


def phase_matrix(k_row, elec_vectors, shape, slab, parts):
    rows, depth = shape
    terms = [k_row[:, d : d + 1] * elec_vectors[d : d + 1, :].astype(jnp.float32) for d in range(3)]
    theta_here = 2.0 * math.pi * (terms[0] + terms[1] + terms[2])
    vector = lax.broadcasted_iota(jnp.int32, (8, depth), 1) // (parts * slab)
    theta = jnp.zeros((8, depth), jnp.float32)
    for e in range(elec_vectors.shape[1]):
        theta = jnp.where(vector == e, theta_here[:, e : e + 1], theta)
    cos = jnp.cos(theta)[:1]
    sin = jnp.sin(theta)[:1]
    row = lax.broadcasted_iota(jnp.int32, shape, 0)
    col = lax.broadcasted_iota(jnp.int32, shape, 1)
    out_part, in_part = row // slab, (col // slab) % parts
    value = jnp.where(out_part == in_part, cos, jnp.where(out_part == 1, sin, -sin))
    return jnp.where(row % slab == col % slab, value, 0.0).astype(jnp.bfloat16)


def partial_kernel(pieces, given, me_ref, *refs):
    table, sems = refs[-2:]
    if given:
        kmat_in, couplings_hbm, *outs = refs[:-2]
    else:
        k_hbm, elec_hbm, couplings_hbm, kmat_out, *outs, k_buf, elec_buf, small = refs[:-2]
        small_copies = [
            pltpu.make_async_copy(k_hbm, k_buf, small.at[0]),
            pltpu.make_async_copy(elec_hbm, elec_buf, small.at[1]),
        ]
        for copy in small_copies:
            copy.start()
    re_here, parts, slab = couplings_hbm.shape[:3]
    rows, depth = parts * slab, re_here * parts * slab
    columns = table.shape[-1]
    copies = []
    for offset, stream, _ in pieces:
        for j in range(HALF):
            place = columns_at(me_ref[0], offset + j, stream, columns)
            n = len(copies)
            copies.append(pltpu.make_async_copy(couplings_hbm.at[:, :, :, place], table.at[n], sems.at[n]))
            copies[-1].start()
    if given:
        kmat = kmat_in[...]
    else:
        for copy in small_copies:
            copy.wait()
        kmat = phase_matrix(k_buf[...], elec_buf[...], (rows, depth), slab, parts)
        kmat_out[...] = kmat
    for n, copy in enumerate(copies):
        out_ref = outs[n // HALF]
        copy.wait()
        flat = table[n].reshape(depth, columns)
        out_ref[n % HALF] = jnp.dot(kmat, flat, preferred_element_type=jnp.float32).astype(out_ref.dtype)


def partial_sums(me, phases, couplings, pieces):
    re_here, parts, slab, width = couplings.shape
    columns = width // BLOCKS
    rows, depth = parts * slab, re_here * parts * slab
    hbm, vmem = pl.BlockSpec(memory_space=pltpu.HBM), pl.BlockSpec(memory_space=pltpu.VMEM)
    given = not isinstance(phases, tuple)
    if given:
        operands, specs, first_out, small = [phases], [vmem], [], []
    else:
        k_point, elec_vectors = phases
        operands = [pltpu.with_memory_space_constraint(a, pltpu.HBM) for a in (k_point.reshape(1, 3), elec_vectors)]
        specs, first_out = [hbm, hbm], [jax.ShapeDtypeStruct((rows, depth), jnp.bfloat16)]
        small = [
            pltpu.VMEM((1, 3), jnp.float32),
            pltpu.VMEM(elec_vectors.shape, jnp.int32),
            pltpu.SemaphoreType.DMA((2,)),
        ]
    copies = HALF * len(pieces)
    outs = first_out + [jax.ShapeDtypeStruct((HALF, rows, columns), dtype) for _, _, dtype in pieces]
    return pl.pallas_call(
        lambda *refs: partial_kernel(pieces, given, *refs),
        in_specs=[pl.BlockSpec(memory_space=pltpu.SMEM), *specs, hbm],
        out_specs=[vmem] * len(outs),
        out_shape=outs,
        scratch_shapes=small
        + [
            pltpu.VMEM((copies, re_here, parts, slab, columns), couplings.dtype),
            pltpu.SemaphoreType.DMA((copies,)),
        ],
        compiler_params=pltpu.CompilerParams(vmem_limit_bytes=VMEM_LIMIT),
        cost_estimate=pl.CostEstimate(
            flops=2 * rows * depth * copies * columns,
            bytes_accessed=2 * depth * copies * columns,
            transcendentals=0,
        ),
    )(me, *operands, pltpu.with_memory_space_constraint(couplings, pltpu.HBM))


def q_matrix_kernel(q_ref, phon_ref, degeneracy_ref, out_ref):
    points, slab = out_ref.shape[0] // 2, out_ref.shape[1] // 2
    dots = lax.dot_general(
        q_ref[...].astype(jnp.float32),
        phon_ref[...].astype(jnp.float32),
        (((0,), (0,)), ((), ())),
        preferred_element_type=jnp.float32,
    )
    wound = jnp.bitwise_and(dots.astype(jnp.int32), NG - 1).astype(jnp.float32)
    angle = 2.0 * math.pi * wound / NG
    weight = 1.0 / degeneracy_ref[...].astype(jnp.float32)
    qcos = jnp.cos(angle) * weight
    qsin = jnp.sin(angle) * weight
    out_ref[:points, :slab] = qcos.astype(out_ref.dtype)
    out_ref[:points, slab:] = (-qsin).astype(out_ref.dtype)
    out_ref[points:, :slab] = qsin.astype(out_ref.dtype)
    out_ref[points:, slab:] = qcos.astype(out_ref.dtype)


def q_matrix(q_index, phon_vectors, degeneracy):
    points, slab = q_index.shape[1], phon_vectors.shape[1]
    return pl.pallas_call(
        q_matrix_kernel,
        out_shape=jax.ShapeDtypeStruct((2 * points, 2 * slab), jnp.bfloat16),
        compiler_params=pltpu.CompilerParams(vmem_limit_bytes=VMEM_LIMIT),
    )(q_index, phon_vectors, degeneracy.reshape(1, slab))


def bloch_kernel(pieces, me_ref, qmat_ref, *refs):
    slabs, (out_hbm, buffer, sems) = refs[: len(pieces)], refs[-3:]
    points, columns = out_hbm.shape[1], buffer.shape[-1]
    copies = []
    for (offset, stream), slab_ref in zip(pieces, slabs):
        for j in range(slab_ref.shape[0]):
            n = len(copies)
            result = jnp.dot(qmat_ref[...], slab_ref[j], preferred_element_type=jnp.float32).astype(buffer.dtype)
            buffer[n, 0] = result[:points]
            buffer[n, 1] = result[points:]
            place = columns_at(me_ref[0], offset + j, stream, columns)
            copies.append(pltpu.make_async_copy(buffer.at[n], out_hbm.at[:, :, place], sems.at[n]))
            copies[-1].start()
    for copy in copies:
        copy.wait()


def bloch(me, qmat, pieces, width, out=None):
    slabs = [slab for slab, _, _ in pieces]
    rows, columns = slabs[0].shape[1:]
    blocks = sum(slab.shape[0] for slab in slabs)
    points = qmat.shape[0] // 2
    vmem, hbm = pl.BlockSpec(memory_space=pltpu.VMEM), pl.BlockSpec(memory_space=pltpu.HBM)
    before = () if out is None else (out,)
    places = [(offset, stream) for _, offset, stream in pieces]
    return pl.pallas_call(
        lambda *refs: bloch_kernel(places, *refs),
        in_specs=[pl.BlockSpec(memory_space=pltpu.SMEM), vmem] + [vmem] * len(slabs) + [hbm] * len(before),
        out_specs=hbm,
        out_shape=jax.ShapeDtypeStruct((2, points, width), jnp.bfloat16),
        scratch_shapes=[
            pltpu.VMEM((blocks, 2, points, columns), jnp.bfloat16),
            pltpu.SemaphoreType.DMA((blocks,)),
        ],
        input_output_aliases={2 + len(slabs): 0} if before else {},
        compiler_params=pltpu.CompilerParams(vmem_limit_bytes=VMEM_LIMIT),
        cost_estimate=pl.CostEstimate(
            flops=4 * points * rows * blocks * columns,
            bytes_accessed=4 * points * blocks * columns,
            transcendentals=0,
        ),
    )(me, qmat, *slabs, *before)


def after(value, *others):
    return lax.optimization_barrier((value, *others))[0]


def on_device(devices, couplings, elec_vectors, phon_vectors, degeneracy, k_point, q_index):
    width = couplings.shape[3]
    wire, full = jnp.bfloat16, jnp.float32
    me = lax.axis_index("blk").astype(jnp.int32).reshape(1)

    def send(array, bits, name):
        with jax.named_scope(name):
            return lax.ppermute(array, "blk", [(i, i ^ bits) for i in range(devices)])

    def to_core(array, name):
        return send(array, 1, name)

    def square(arrays, name):
        return [send(a, bits, name) for a, bits in zip(arrays, (2, 4, 6))]

    def added(own, got):
        for array in got:
            own = own + array.astype(full)
        return own

    def far_sum(own, name):
        step = 8
        while step < devices:
            own = own + send(own.astype(wire), step, name).astype(full)
            step *= 2
        return own.astype(wire)

    kmat, p_theirs = partial_sums(me, (k_point, elec_vectors), couplings, [(0, 0, wire)])
    p_got = to_core(p_theirs, "p_core")
    p_own, q_theirs = partial_sums(me, kmat, couplings, [(HALF, 0, full), (0, 1, wire)])
    q_got = to_core(q_theirs, "q_core")
    p_sum = p_own + p_got.astype(full)
    p_first = [p_sum[i : i + 1].astype(wire) for i in (1, 2, 0)]
    p_got = square(p_first, "p_rs")

    (q_own,) = partial_sums(after(me, p_first[0]), kmat, couplings, [(HALF, 1, full)])
    qmat = q_matrix(after(q_index, p_first[0]), phon_vectors, degeneracy)
    q_own = after(q_own, qmat)
    q_sum = q_own + q_got.astype(full)
    q_first = [q_sum[i : i + 1].astype(wire) for i in (1, 2, 0)]
    q_got = square(q_first, "q_rs")

    p_block = far_sum(added(p_sum[3:], p_got), "p_far")
    q_block = far_sum(added(q_sum[3:], q_got), "q_far")

    p_got = square([p_block] * 3, "p_ag")
    q_got = square([q_block] * 3, "q_ag")

    p_quad = jnp.concatenate([p_got[2], p_got[0], p_got[1], p_block])
    out = bloch(me, qmat, [(p_quad, HALF, 0)], width)
    p_rest = to_core(p_quad, "p_core2")

    q_got[0] = after(q_got[0], out)
    q_quad = jnp.concatenate([q_got[2], q_got[0], q_got[1], q_block])
    q_rest = to_core(q_quad, "q_core2")
    out = bloch(me, qmat, [(p_rest, 0, 0), (q_quad, HALF, 1)], width, out)
    return bloch(me, qmat, [(q_rest, 0, 1)], width, out)


def solution(mesh):
    placed = (
        P("blk", None, "grp", None),
        P(None, "blk"),
        P(None, "grp"),
        P("grp"),
        P("grp"),
        P(None, "blk"),
    )
    devices = mesh.shape["blk"]
    return jax.shard_map(
        lambda *arrays: on_device(devices, *arrays),
        mesh=mesh,
        in_specs=placed,
        out_specs=P(None, ("grp", "blk"), None),
        check_vma=False,
    )
```

```python
import math

import jax
import jax.numpy as jnp
from jax import lax
from jax.experimental import pallas as pl
from jax.experimental.pallas import tpu as pltpu
from jax.sharding import PartitionSpec as P

NG = 16
STREAMS = (1, 1)
BLOCKS = 8
SHARE = (1, 3)
LANES = 128
VMEM_LIMIT = 24 * 2**20

CHIPS = ("across", "x", "z", "own")
SQUARE = (6, 2, 4)
SUM_ORDER = (1, 2, 0)
GATHER_ORDER = (1, 2, 0)


def block_of(me, place):
    other, chip = place
    core, x, z = me % 2, (me // 2) % 2, (me // 4) % 2
    flip_x, flip_z = {"across": (1, 1), "x": (1, 0), "z": (0, 1), "own": (0, 0)}[chip]
    return (core + other) % 2 * 4 + (x + flip_x) % 2 * 2 + (z + flip_z) % 2


def stream_columns(width, stream):
    unit = width // BLOCKS // sum(STREAMS)
    return sum(STREAMS[:stream]) * unit * BLOCKS, STREAMS[stream] * unit


def columns_at(me, place, stream, width):
    start, columns = stream_columns(width, stream)
    start = start + block_of(me, place) * columns
    return pl.ds(pl.multiple_of(start, 128), columns)


def phase_matrix(k_row, elec_vectors, shape, slab, parts):
    rows, depth = shape
    terms = [k_row[:, d : d + 1] * elec_vectors[d : d + 1, :].astype(jnp.float32) for d in range(3)]
    theta_here = 2.0 * math.pi * (terms[0] + terms[1] + terms[2])
    vector = lax.broadcasted_iota(jnp.int32, (8, depth), 1) // (parts * slab)
    theta = jnp.zeros((8, depth), jnp.float32)
    for e in range(elec_vectors.shape[1]):
        theta = jnp.where(vector == e, theta_here[:, e : e + 1], theta)
    cos = jnp.cos(theta)[:1]
    sin = jnp.sin(theta)[:1]
    row = lax.broadcasted_iota(jnp.int32, shape, 0)
    col = lax.broadcasted_iota(jnp.int32, shape, 1)
    out_part, in_part = row // slab, (col // slab) % parts
    value = jnp.where(out_part == in_part, cos, jnp.where(out_part == 1, sin, -sin))
    return jnp.where(row % slab == col % slab, value, 0.0).astype(jnp.bfloat16)


def partial_kernel(pieces, given, me_ref, *refs):
    *refs, sems = refs
    refs, tables = refs[: -len(pieces)], refs[-len(pieces) :]
    if given:
        kmat_in, couplings_hbm, *outs = refs
    else:
        k_hbm, elec_hbm, couplings_hbm, kmat_out, *outs, k_buf, elec_buf, small = refs
        small_copies = [
            pltpu.make_async_copy(k_hbm, k_buf, small.at[0]),
            pltpu.make_async_copy(elec_hbm, elec_buf, small.at[1]),
        ]
        for copy in small_copies:
            copy.start()
    re_here, parts, slab = couplings_hbm.shape[:3]
    rows, depth = parts * slab, re_here * parts * slab
    width = couplings_hbm.shape[3]
    copies = []
    for piece, (other, stream, _) in enumerate(pieces):
        for j, chip in enumerate(CHIPS):
            place = columns_at(me_ref[0], (other, chip), stream, width)
            n = len(copies)
            copies.append(pltpu.make_async_copy(couplings_hbm.at[:, :, :, place], tables[piece].at[j], sems.at[n]))
            copies[-1].start()
    if given:
        kmat = kmat_in[...]
    else:
        for copy in small_copies:
            copy.wait()
        kmat = phase_matrix(k_buf[...], elec_buf[...], (rows, depth), slab, parts)
        kmat_out[...] = kmat
    here = [
        tuple(kmat[r : r + 1, e * rows : e * rows + 1].astype(jnp.float32) for r in (0, slab)) for e in range(re_here)
    ]
    for n, copy in enumerate(copies):
        out_ref, table = outs[n // len(CHIPS)], tables[n // len(CHIPS)]
        columns = out_ref.shape[-1]
        split = columns * SHARE[0] // SHARE[1] // 128 * 128
        copy.wait()
        if split:
            flat = table[n % len(CHIPS), :, :, :, :split].reshape(depth, split)
            out_ref[n % len(CHIPS), :, :split] = jnp.dot(kmat, flat, preferred_element_type=jnp.float32).astype(out_ref.dtype)
        for low in range(split, columns, LANES):
            place = pl.ds(low, min(LANES, columns - low))
            real = imag = 0.0
            for e, (cos, sin) in enumerate(here):
                a = table[n % len(CHIPS), e, 0, :, place].astype(jnp.float32)
                b = table[n % len(CHIPS), e, 1, :, place].astype(jnp.float32)
                real, imag = real + (cos * a - sin * b), imag + (sin * a + cos * b)
            out_ref[n % len(CHIPS), :slab, place] = real.astype(out_ref.dtype)
            out_ref[n % len(CHIPS), slab:, place] = imag.astype(out_ref.dtype)


def partial_sums(me, phases, couplings, pieces):
    re_here, parts, slab, width = couplings.shape
    sizes = [stream_columns(width, stream)[1] for _, stream, _ in pieces]
    rows, depth = parts * slab, re_here * parts * slab
    hbm, vmem = pl.BlockSpec(memory_space=pltpu.HBM), pl.BlockSpec(memory_space=pltpu.VMEM)
    given = not isinstance(phases, tuple)
    if given:
        operands, specs, first_out, small = [phases], [vmem], [], []
    else:
        k_point, elec_vectors = phases
        operands = [pltpu.with_memory_space_constraint(a, pltpu.HBM) for a in (k_point.reshape(1, 3), elec_vectors)]
        specs, first_out = [hbm, hbm], [jax.ShapeDtypeStruct((rows, depth), jnp.bfloat16)]
        small = [
            pltpu.VMEM((1, 3), jnp.float32),
            pltpu.VMEM(elec_vectors.shape, jnp.int32),
            pltpu.SemaphoreType.DMA((2,)),
        ]
    copies = len(CHIPS) * len(pieces)
    outs = first_out + [jax.ShapeDtypeStruct((len(CHIPS), rows, n), dtype) for (_, _, dtype), n in zip(pieces, sizes)]
    return pl.pallas_call(
        lambda *refs: partial_kernel(pieces, given, *refs),
        in_specs=[pl.BlockSpec(memory_space=pltpu.SMEM), *specs, hbm],
        out_specs=[vmem] * len(outs),
        out_shape=outs,
        scratch_shapes=small
        + [pltpu.VMEM((len(CHIPS), re_here, parts, slab, n), couplings.dtype) for n in sizes]
        + [pltpu.SemaphoreType.DMA((copies,))],
        compiler_params=pltpu.CompilerParams(vmem_limit_bytes=VMEM_LIMIT),
        cost_estimate=pl.CostEstimate(
            flops=2 * rows * depth * len(CHIPS) * sum(sizes),
            bytes_accessed=2 * depth * len(CHIPS) * sum(sizes),
            transcendentals=0,
        ),
    )(me, *operands, pltpu.with_memory_space_constraint(couplings, pltpu.HBM))


def q_matrix_kernel(q_ref, phon_ref, degeneracy_ref, out_ref):
    points, slab = out_ref.shape[0] // 2, out_ref.shape[1] // 2
    dots = lax.dot_general(
        q_ref[...].astype(jnp.float32),
        phon_ref[...].astype(jnp.float32),
        (((0,), (0,)), ((), ())),
        preferred_element_type=jnp.float32,
    )
    wound = jnp.bitwise_and(dots.astype(jnp.int32), NG - 1).astype(jnp.float32)
    angle = 2.0 * math.pi * wound / NG
    weight = 1.0 / degeneracy_ref[...].astype(jnp.float32)
    qcos = jnp.cos(angle) * weight
    qsin = jnp.sin(angle) * weight
    out_ref[:points, :slab] = qcos.astype(out_ref.dtype)
    out_ref[:points, slab:] = (-qsin).astype(out_ref.dtype)
    out_ref[points:, :slab] = qsin.astype(out_ref.dtype)
    out_ref[points:, slab:] = qcos.astype(out_ref.dtype)


def q_matrix(q_index, phon_vectors, degeneracy):
    points, slab = q_index.shape[1], phon_vectors.shape[1]
    return pl.pallas_call(
        q_matrix_kernel,
        out_shape=jax.ShapeDtypeStruct((2 * points, 2 * slab), jnp.bfloat16),
        compiler_params=pltpu.CompilerParams(vmem_limit_bytes=VMEM_LIMIT),
    )(q_index, phon_vectors, degeneracy.reshape(1, slab))


def bloch_kernel(places, me_ref, qmat_ref, *refs):
    count = len(places)
    slabs, out_hbm, buffers, sems = refs[:count], refs[-count - 2], refs[-count - 1 : -1], refs[-1]
    points, width = out_hbm.shape[1:]
    copies = []
    for (other, stream), slab_ref, buffer in zip(places, slabs, buffers):
        for j, chip in enumerate(CHIPS):
            result = jnp.dot(qmat_ref[...], slab_ref[j], preferred_element_type=jnp.float32).astype(buffer.dtype)
            buffer[j, 0] = result[:points]
            buffer[j, 1] = result[points:]
            place = columns_at(me_ref[0], (other, chip), stream, width)
            copies.append(pltpu.make_async_copy(buffer.at[j], out_hbm.at[:, :, place], sems.at[len(copies)]))
            copies[-1].start()
    for copy in copies:
        copy.wait()


def bloch(me, qmat, pieces, width, out=None):
    slabs = [slab for slab, _, _ in pieces]
    places = [(other, stream) for _, other, stream in pieces]
    columns = sum(slab.shape[0] * slab.shape[2] for slab in slabs)
    points = qmat.shape[0] // 2
    vmem, hbm = pl.BlockSpec(memory_space=pltpu.VMEM), pl.BlockSpec(memory_space=pltpu.HBM)
    before = () if out is None else (out,)
    return pl.pallas_call(
        lambda *refs: bloch_kernel(places, *refs),
        in_specs=[pl.BlockSpec(memory_space=pltpu.SMEM), vmem] + [vmem] * len(slabs) + [hbm] * len(before),
        out_specs=hbm,
        out_shape=jax.ShapeDtypeStruct((2, points, width), jnp.bfloat16),
        scratch_shapes=[pltpu.VMEM((slab.shape[0], 2, points, slab.shape[2]), jnp.bfloat16) for slab in slabs]
        + [pltpu.SemaphoreType.DMA((sum(slab.shape[0] for slab in slabs),))],
        input_output_aliases={2 + len(slabs): 0} if before else {},
        compiler_params=pltpu.CompilerParams(vmem_limit_bytes=VMEM_LIMIT),
        cost_estimate=pl.CostEstimate(
            flops=2 * qmat.size * columns,
            bytes_accessed=4 * points * columns,
            transcendentals=0,
        ),
    )(me, qmat, *slabs, *before)


def after(value, *others):
    return lax.optimization_barrier((value, *others))[0]


def on_device(devices, couplings, elec_vectors, phon_vectors, degeneracy, k_point, q_index):
    width = couplings.shape[3]
    wire, full = jnp.bfloat16, jnp.float32
    me = lax.axis_index("blk").astype(jnp.int32).reshape(1)
    streams = range(len(STREAMS))
    last = len(STREAMS) - 1

    def send(array, bits, name):
        with jax.named_scope(name):
            return lax.ppermute(array, "blk", [(i, i ^ bits) for i in range(devices)])

    def to_core(array, name):
        return send(array, 1, name)

    got, first, total, block = {}, {}, {}, {}
    kmat, theirs = partial_sums(me, (k_point, elec_vectors), couplings, [(1, 0, wire)])
    got[0] = to_core(theirs, "core_sum0")
    for s in streams:
        here = me if s == 0 else after(me, first[s - 1])
        pieces = [(0, s, full)] + [(1, s + 1, wire)] * (s < last)
        own, *theirs = partial_sums(here, kmat, couplings, pieces)
        if theirs:
            got[s + 1] = to_core(theirs[0], f"core_sum{s + 1}")
        total[s] = own + got[s].astype(full)
        parts = [total[s][i : i + 1].astype(wire) for i in SUM_ORDER]
        first[s] = parts[0]
        got[s] = [send(part, SQUARE[i], f"square_sum{s}") for i, part in zip(SUM_ORDER, parts)]
    qmat = q_matrix(after(q_index, first[last]), phon_vectors, degeneracy)
    total[last] = after(total[last], qmat)

    for s in streams:
        own = total[s][3:]
        for array in got[s]:
            own = own + array.astype(full)
        step = 8
        while step < devices:
            own = own + send(own.astype(wire), step, f"far_sum{s}").astype(full)
            step *= 2
        block[s] = own.astype(wire)

    for s in streams:
        back = {i: send(block[s], SQUARE[i], f"square_gather{s}") for i in GATHER_ORDER}
        got[s] = [back[i] for i in range(3)]

    out = None
    for s in streams:
        if s:
            got[s][0] = after(got[s][0], out)
        mine = jnp.concatenate([*got[s], block[s]])
        pieces = [(mine, 0, s)] if s == 0 else [(theirs, 1, s - 1), (mine, 0, s)]
        theirs = to_core(mine, f"core_gather{s}")
        out = bloch(me, qmat, pieces, width, out)
    return bloch(me, qmat, [(theirs, 1, last)], width, out)


def solution(mesh):
    placed = (
        P("blk", None, "grp", None),
        P(None, "blk"),
        P(None, "grp"),
        P("grp"),
        P("grp"),
        P(None, "blk"),
    )
    devices = mesh.shape["blk"]
    return jax.shard_map(
        lambda *arrays: on_device(devices, *arrays),
        mesh=mesh,
        in_specs=placed,
        out_specs=P(None, ("grp", "blk"), None),
        check_vma=False,
    )
```

```python
import math

import jax
import jax.numpy as jnp
from jax import lax
from jax.experimental import pallas as pl
from jax.experimental.pallas import tpu as pltpu
from jax.sharding import PartitionSpec as P

NG = 16
STREAMS = (1, 1)
BLOCKS = 8
SHARE = (1, 4)
LANES = 128
VMEM_LIMIT = 24 * 2**20

CHIPS = ("across", "x", "z", "own")
SQUARE = (6, 2, 4)
SUM_ORDER = (2, 1, 0)
GATHER_ORDER = (2, 1, 0)


def block_of(me, place):
    other, chip = place
    core, x, z = me % 2, (me // 2) % 2, (me // 4) % 2
    flip_x, flip_z = {"across": (1, 1), "x": (1, 0), "z": (0, 1), "own": (0, 0)}[chip]
    return (core + other) % 2 * 4 + (x + flip_x) % 2 * 2 + (z + flip_z) % 2


def stream_columns(width, stream):
    unit = width // BLOCKS // sum(STREAMS)
    return sum(STREAMS[:stream]) * unit * BLOCKS, STREAMS[stream] * unit


def columns_at(me, place, stream, width):
    start, columns = stream_columns(width, stream)
    start = start + block_of(me, place) * columns
    return pl.ds(pl.multiple_of(start, 128), columns)


def phase_matrix(k_row, elec_vectors, shape, slab, parts):
    rows, depth = shape
    terms = [k_row[:, d : d + 1] * elec_vectors[d : d + 1, :].astype(jnp.float32) for d in range(3)]
    theta_here = 2.0 * math.pi * (terms[0] + terms[1] + terms[2])
    vector = lax.broadcasted_iota(jnp.int32, (8, depth), 1) // (parts * slab)
    theta = jnp.zeros((8, depth), jnp.float32)
    for e in range(elec_vectors.shape[1]):
        theta = jnp.where(vector == e, theta_here[:, e : e + 1], theta)
    cos = jnp.cos(theta)[:1]
    sin = jnp.sin(theta)[:1]
    row = lax.broadcasted_iota(jnp.int32, shape, 0)
    col = lax.broadcasted_iota(jnp.int32, shape, 1)
    out_part, in_part = row // slab, (col // slab) % parts
    value = jnp.where(out_part == in_part, cos, jnp.where(out_part == 1, sin, -sin))
    return jnp.where(row % slab == col % slab, value, 0.0).astype(jnp.bfloat16)


def partial_kernel(pieces, given, me_ref, *refs):
    *refs, sems = refs
    refs, tables = refs[: -len(pieces)], refs[-len(pieces) :]
    if given:
        kmat_in, couplings_hbm, *outs = refs
    else:
        k_hbm, elec_hbm, couplings_hbm, kmat_out, *outs, k_buf, elec_buf, small = refs
        small_copies = [
            pltpu.make_async_copy(k_hbm, k_buf, small.at[0]),
            pltpu.make_async_copy(elec_hbm, elec_buf, small.at[1]),
        ]
        for copy in small_copies:
            copy.start()
    re_here, parts, slab = couplings_hbm.shape[:3]
    rows, depth = parts * slab, re_here * parts * slab
    width = couplings_hbm.shape[3]
    copies = []
    for piece, (other, stream, _) in enumerate(pieces):
        for j, chip in enumerate(CHIPS):
            place = columns_at(me_ref[0], (other, chip), stream, width)
            n = len(copies)
            copies.append(pltpu.make_async_copy(couplings_hbm.at[:, :, :, place], tables[piece].at[j], sems.at[n]))
            copies[-1].start()
    if given:
        kmat = kmat_in[...]
    else:
        for copy in small_copies:
            copy.wait()
        kmat = phase_matrix(k_buf[...], elec_buf[...], (rows, depth), slab, parts)
        kmat_out[...] = kmat
    here = [
        tuple(kmat[r : r + 1, e * rows : e * rows + 1].astype(jnp.float32) for r in (0, slab)) for e in range(re_here)
    ]
    for n, copy in enumerate(copies):
        out_ref, table = outs[n // len(CHIPS)], tables[n // len(CHIPS)]
        columns = out_ref.shape[-1]
        split = columns * SHARE[0] // SHARE[1] // 128 * 128
        copy.wait()
        if split:
            flat = table[n % len(CHIPS), :, :, :, :split].reshape(depth, split)
            out_ref[n % len(CHIPS), :, :split] = jnp.dot(kmat, flat, preferred_element_type=jnp.float32).astype(out_ref.dtype)
        for low in range(split, columns, LANES):
            place = pl.ds(low, min(LANES, columns - low))
            real = imag = 0.0
            for e, (cos, sin) in enumerate(here):
                a = table[n % len(CHIPS), e, 0, :, place].astype(jnp.float32)
                b = table[n % len(CHIPS), e, 1, :, place].astype(jnp.float32)
                real, imag = real + (cos * a - sin * b), imag + (sin * a + cos * b)
            out_ref[n % len(CHIPS), :slab, place] = real.astype(out_ref.dtype)
            out_ref[n % len(CHIPS), slab:, place] = imag.astype(out_ref.dtype)


def partial_sums(me, phases, couplings, pieces):
    re_here, parts, slab, width = couplings.shape
    sizes = [stream_columns(width, stream)[1] for _, stream, _ in pieces]
    rows, depth = parts * slab, re_here * parts * slab
    hbm, vmem = pl.BlockSpec(memory_space=pltpu.HBM), pl.BlockSpec(memory_space=pltpu.VMEM)
    given = not isinstance(phases, tuple)
    if given:
        operands, specs, first_out, small = [phases], [vmem], [], []
    else:
        k_point, elec_vectors = phases
        operands = [pltpu.with_memory_space_constraint(a, pltpu.HBM) for a in (k_point.reshape(1, 3), elec_vectors)]
        specs, first_out = [hbm, hbm], [jax.ShapeDtypeStruct((rows, depth), jnp.bfloat16)]
        small = [
            pltpu.VMEM((1, 3), jnp.float32),
            pltpu.VMEM(elec_vectors.shape, jnp.int32),
            pltpu.SemaphoreType.DMA((2,)),
        ]
    copies = len(CHIPS) * len(pieces)
    outs = first_out + [jax.ShapeDtypeStruct((len(CHIPS), rows, n), dtype) for (_, _, dtype), n in zip(pieces, sizes)]
    return pl.pallas_call(
        lambda *refs: partial_kernel(pieces, given, *refs),
        in_specs=[pl.BlockSpec(memory_space=pltpu.SMEM), *specs, hbm],
        out_specs=[vmem] * len(outs),
        out_shape=outs,
        scratch_shapes=small
        + [pltpu.VMEM((len(CHIPS), re_here, parts, slab, n), couplings.dtype) for n in sizes]
        + [pltpu.SemaphoreType.DMA((copies,))],
        compiler_params=pltpu.CompilerParams(vmem_limit_bytes=VMEM_LIMIT),
        cost_estimate=pl.CostEstimate(
            flops=2 * rows * depth * len(CHIPS) * sum(sizes),
            bytes_accessed=2 * depth * len(CHIPS) * sum(sizes),
            transcendentals=0,
        ),
    )(me, *operands, pltpu.with_memory_space_constraint(couplings, pltpu.HBM))


def q_matrix_kernel(q_ref, phon_ref, degeneracy_ref, out_ref):
    points, slab = out_ref.shape[0] // 2, out_ref.shape[1] // 2
    dots = lax.dot_general(
        q_ref[...].astype(jnp.float32),
        phon_ref[...].astype(jnp.float32),
        (((0,), (0,)), ((), ())),
        preferred_element_type=jnp.float32,
    )
    wound = jnp.bitwise_and(dots.astype(jnp.int32), NG - 1).astype(jnp.float32)
    angle = 2.0 * math.pi * wound / NG
    weight = 1.0 / degeneracy_ref[...].astype(jnp.float32)
    qcos = jnp.cos(angle) * weight
    qsin = jnp.sin(angle) * weight
    out_ref[:points, :slab] = qcos.astype(out_ref.dtype)
    out_ref[:points, slab:] = (-qsin).astype(out_ref.dtype)
    out_ref[points:, :slab] = qsin.astype(out_ref.dtype)
    out_ref[points:, slab:] = qcos.astype(out_ref.dtype)


def q_matrix(q_index, phon_vectors, degeneracy):
    points, slab = q_index.shape[1], phon_vectors.shape[1]
    return pl.pallas_call(
        q_matrix_kernel,
        out_shape=jax.ShapeDtypeStruct((2 * points, 2 * slab), jnp.bfloat16),
        compiler_params=pltpu.CompilerParams(vmem_limit_bytes=VMEM_LIMIT),
    )(q_index, phon_vectors, degeneracy.reshape(1, slab))


def bloch_kernel(places, me_ref, qmat_ref, *refs):
    count = len(places)
    slabs, out_hbm, buffers, sems = refs[:count], refs[-count - 2], refs[-count - 1 : -1], refs[-1]
    points, width = out_hbm.shape[1:]
    copies = []
    for (other, stream), slab_ref, buffer in zip(places, slabs, buffers):
        for j, chip in enumerate(CHIPS):
            result = jnp.dot(qmat_ref[...], slab_ref[j], preferred_element_type=jnp.float32).astype(buffer.dtype)
            buffer[j, 0] = result[:points]
            buffer[j, 1] = result[points:]
            place = columns_at(me_ref[0], (other, chip), stream, width)
            copies.append(pltpu.make_async_copy(buffer.at[j], out_hbm.at[:, :, place], sems.at[len(copies)]))
            copies[-1].start()
    for copy in copies:
        copy.wait()


def bloch(me, qmat, pieces, width, out=None):
    slabs = [slab for slab, _, _ in pieces]
    places = [(other, stream) for _, other, stream in pieces]
    columns = sum(slab.shape[0] * slab.shape[2] for slab in slabs)
    points = qmat.shape[0] // 2
    vmem, hbm = pl.BlockSpec(memory_space=pltpu.VMEM), pl.BlockSpec(memory_space=pltpu.HBM)
    before = () if out is None else (out,)
    return pl.pallas_call(
        lambda *refs: bloch_kernel(places, *refs),
        in_specs=[pl.BlockSpec(memory_space=pltpu.SMEM), vmem] + [vmem] * len(slabs) + [hbm] * len(before),
        out_specs=hbm,
        out_shape=jax.ShapeDtypeStruct((2, points, width), jnp.bfloat16),
        scratch_shapes=[pltpu.VMEM((slab.shape[0], 2, points, slab.shape[2]), jnp.bfloat16) for slab in slabs]
        + [pltpu.SemaphoreType.DMA((sum(slab.shape[0] for slab in slabs),))],
        input_output_aliases={2 + len(slabs): 0} if before else {},
        compiler_params=pltpu.CompilerParams(vmem_limit_bytes=VMEM_LIMIT),
        cost_estimate=pl.CostEstimate(
            flops=2 * qmat.size * columns,
            bytes_accessed=4 * points * columns,
            transcendentals=0,
        ),
    )(me, qmat, *slabs, *before)


def after(value, *others):
    return lax.optimization_barrier((value, *others))[0]


def on_device(devices, couplings, elec_vectors, phon_vectors, degeneracy, k_point, q_index):
    width = couplings.shape[3]
    wire, full = jnp.bfloat16, jnp.float32
    me = lax.axis_index("blk").astype(jnp.int32).reshape(1)
    streams = range(len(STREAMS))
    last = len(STREAMS) - 1

    def send(array, bits, name):
        with jax.named_scope(name):
            return lax.ppermute(array, "blk", [(i, i ^ bits) for i in range(devices)])

    def to_core(array, name):
        return send(array, 1, name)

    got, first, total, block = {}, {}, {}, {}
    kmat, theirs = partial_sums(me, (k_point, elec_vectors), couplings, [(1, 0, wire)])
    got[0] = to_core(theirs, "core_sum0")
    for s in streams:
        here = me if s == 0 else after(me, first[s - 1])
        pieces = [(0, s, full)] + [(1, s + 1, wire)] * (s < last)
        own, *theirs = partial_sums(here, kmat, couplings, pieces)
        if theirs:
            got[s + 1] = to_core(theirs[0], f"core_sum{s + 1}")
        total[s] = own + got[s].astype(full)
        parts = [total[s][i : i + 1].astype(wire) for i in SUM_ORDER]
        first[s] = parts[0]
        got[s] = [send(part, SQUARE[i], f"square_sum{s}") for i, part in zip(SUM_ORDER, parts)]
    for s in streams:
        own = total[s][3:]
        if s == last:
            qmat = q_matrix(after(q_index, early), phon_vectors, degeneracy)
            own = after(own, qmat)
        for array in got[s]:
            own = own + array.astype(full)
        early = own.astype(wire)
        step = 8
        while step < devices:
            own = own + send(own.astype(wire), step, f"far_sum{s}").astype(full)
            step *= 2
        block[s] = own.astype(wire)

    for s in streams:
        back = {i: send(block[s], SQUARE[i], f"square_gather{s}") for i in GATHER_ORDER}
        got[s] = [back[i] for i in range(3)]

    out = None
    for s in streams:
        if s:
            got[s][0] = after(got[s][0], out)
        mine = jnp.concatenate([*got[s], block[s]])
        pieces = [(mine, 0, s)] if s == 0 else [(theirs, 1, s - 1), (mine, 0, s)]
        theirs = to_core(mine, f"core_gather{s}")
        out = bloch(me, qmat, pieces, width, out)
    return bloch(me, qmat, [(theirs, 1, last)], width, out)


def solution(mesh):
    placed = (
        P("blk", None, "grp", None),
        P(None, "blk"),
        P(None, "grp"),
        P("grp"),
        P("grp"),
        P(None, "blk"),
    )
    devices = mesh.shape["blk"]
    return jax.shard_map(
        lambda *arrays: on_device(devices, *arrays),
        mesh=mesh,
        in_specs=placed,
        out_specs=P(None, ("grp", "blk"), None),
        check_vma=False,
    )
```

```python
import math

import jax
import jax.numpy as jnp
from jax import lax
from jax.experimental import pallas as pl
from jax.experimental.pallas import tpu as pltpu
from jax.sharding import PartitionSpec as P

NG = 16
STREAMS = (1, 1)
BLOCKS = 8
SHARE = (1, 4)
LANES = 128
VMEM_LIMIT = 24 * 2**20

CHIPS = ("across", "x", "z", "own")
SQUARE = (6, 2, 4)
SUM_ORDER = (2, 0, 1)
GATHER_ORDER = (2, 0, 1)
MIRROR = (0, 1)


def block_of(me, place, stream):
    other, chip = place
    core, x, z = me % 2, (me // 2) % 2, (me // 4 + MIRROR[stream] * (me // 8)) % 2
    flip_x, flip_z = {"across": (1, 1), "x": (1, 0), "z": (0, 1), "own": (0, 0)}[chip]
    return (core + other) % 2 * 4 + (x + flip_x) % 2 * 2 + (z + flip_z) % 2


def stream_columns(width, stream):
    unit = width // BLOCKS // sum(STREAMS)
    return sum(STREAMS[:stream]) * unit * BLOCKS, STREAMS[stream] * unit


def columns_at(me, place, stream, width):
    start, columns = stream_columns(width, stream)
    start = start + block_of(me, place, stream) * columns
    return pl.ds(pl.multiple_of(start, 128), columns)


def phase_matrix(k_row, elec_vectors, shape, slab, parts):
    rows, depth = shape
    terms = [k_row[:, d : d + 1] * elec_vectors[d : d + 1, :].astype(jnp.float32) for d in range(3)]
    theta_here = 2.0 * math.pi * (terms[0] + terms[1] + terms[2])
    vector = lax.broadcasted_iota(jnp.int32, (8, depth), 1) // (parts * slab)
    theta = jnp.zeros((8, depth), jnp.float32)
    for e in range(elec_vectors.shape[1]):
        theta = jnp.where(vector == e, theta_here[:, e : e + 1], theta)
    cos = jnp.cos(theta)[:1]
    sin = jnp.sin(theta)[:1]
    row = lax.broadcasted_iota(jnp.int32, shape, 0)
    col = lax.broadcasted_iota(jnp.int32, shape, 1)
    out_part, in_part = row // slab, (col // slab) % parts
    value = jnp.where(out_part == in_part, cos, jnp.where(out_part == 1, sin, -sin))
    return jnp.where(row % slab == col % slab, value, 0.0).astype(jnp.bfloat16)


def partial_kernel(pieces, given, me_ref, *refs):
    *refs, sems = refs
    refs, tables = refs[: -len(pieces)], refs[-len(pieces) :]
    if given:
        kmat_in, couplings_hbm, *outs = refs
    else:
        k_hbm, elec_hbm, couplings_hbm, kmat_out, *outs, k_buf, elec_buf, small = refs
        small_copies = [
            pltpu.make_async_copy(k_hbm, k_buf, small.at[0]),
            pltpu.make_async_copy(elec_hbm, elec_buf, small.at[1]),
        ]
        for copy in small_copies:
            copy.start()
    re_here, parts, slab = couplings_hbm.shape[:3]
    rows, depth = parts * slab, re_here * parts * slab
    width = couplings_hbm.shape[3]
    copies = []
    for piece, (other, stream, _) in enumerate(pieces):
        for j, chip in enumerate(CHIPS):
            place = columns_at(me_ref[0], (other, chip), stream, width)
            n = len(copies)
            copies.append(pltpu.make_async_copy(couplings_hbm.at[:, :, :, place], tables[piece].at[j], sems.at[n]))
            copies[-1].start()
    if given:
        kmat = kmat_in[...]
    else:
        for copy in small_copies:
            copy.wait()
        kmat = phase_matrix(k_buf[...], elec_buf[...], (rows, depth), slab, parts)
        kmat_out[...] = kmat
    here = [
        tuple(kmat[r : r + 1, e * rows : e * rows + 1].astype(jnp.float32) for r in (0, slab)) for e in range(re_here)
    ]
    for n, copy in enumerate(copies):
        out_ref, table = outs[n // len(CHIPS)], tables[n // len(CHIPS)]
        columns = out_ref.shape[-1]
        split = columns * SHARE[0] // SHARE[1] // 128 * 128
        copy.wait()
        if split:
            flat = table[n % len(CHIPS), :, :, :, :split].reshape(depth, split)
            out_ref[n % len(CHIPS), :, :split] = jnp.dot(kmat, flat, preferred_element_type=jnp.float32).astype(out_ref.dtype)
        for low in range(split, columns, LANES):
            place = pl.ds(low, min(LANES, columns - low))
            real = imag = 0.0
            for e, (cos, sin) in enumerate(here):
                a = table[n % len(CHIPS), e, 0, :, place].astype(jnp.float32)
                b = table[n % len(CHIPS), e, 1, :, place].astype(jnp.float32)
                real, imag = real + (cos * a - sin * b), imag + (sin * a + cos * b)
            out_ref[n % len(CHIPS), :slab, place] = real.astype(out_ref.dtype)
            out_ref[n % len(CHIPS), slab:, place] = imag.astype(out_ref.dtype)


def partial_sums(me, phases, couplings, pieces):
    re_here, parts, slab, width = couplings.shape
    sizes = [stream_columns(width, stream)[1] for _, stream, _ in pieces]
    rows, depth = parts * slab, re_here * parts * slab
    hbm, vmem = pl.BlockSpec(memory_space=pltpu.HBM), pl.BlockSpec(memory_space=pltpu.VMEM)
    given = not isinstance(phases, tuple)
    if given:
        operands, specs, first_out, small = [phases], [vmem], [], []
    else:
        k_point, elec_vectors = phases
        operands = [pltpu.with_memory_space_constraint(a, pltpu.HBM) for a in (k_point.reshape(1, 3), elec_vectors)]
        specs, first_out = [hbm, hbm], [jax.ShapeDtypeStruct((rows, depth), jnp.bfloat16)]
        small = [
            pltpu.VMEM((1, 3), jnp.float32),
            pltpu.VMEM(elec_vectors.shape, jnp.int32),
            pltpu.SemaphoreType.DMA((2,)),
        ]
    copies = len(CHIPS) * len(pieces)
    outs = first_out + [jax.ShapeDtypeStruct((len(CHIPS), rows, n), dtype) for (_, _, dtype), n in zip(pieces, sizes)]
    return pl.pallas_call(
        lambda *refs: partial_kernel(pieces, given, *refs),
        in_specs=[pl.BlockSpec(memory_space=pltpu.SMEM), *specs, hbm],
        out_specs=[vmem] * len(outs),
        out_shape=outs,
        scratch_shapes=small
        + [pltpu.VMEM((len(CHIPS), re_here, parts, slab, n), couplings.dtype) for n in sizes]
        + [pltpu.SemaphoreType.DMA((copies,))],
        compiler_params=pltpu.CompilerParams(vmem_limit_bytes=VMEM_LIMIT),
        cost_estimate=pl.CostEstimate(
            flops=2 * rows * depth * len(CHIPS) * sum(sizes),
            bytes_accessed=2 * depth * len(CHIPS) * sum(sizes),
            transcendentals=0,
        ),
    )(me, *operands, pltpu.with_memory_space_constraint(couplings, pltpu.HBM))


def q_matrix_kernel(q_ref, phon_ref, degeneracy_ref, out_ref):
    points, slab = out_ref.shape[0] // 2, out_ref.shape[1] // 2
    dots = lax.dot_general(
        q_ref[...].astype(jnp.float32),
        phon_ref[...].astype(jnp.float32),
        (((0,), (0,)), ((), ())),
        preferred_element_type=jnp.float32,
    )
    wound = jnp.bitwise_and(dots.astype(jnp.int32), NG - 1).astype(jnp.float32)
    angle = 2.0 * math.pi * wound / NG
    weight = 1.0 / degeneracy_ref[...].astype(jnp.float32)
    qcos = jnp.cos(angle) * weight
    qsin = jnp.sin(angle) * weight
    out_ref[:points, :slab] = qcos.astype(out_ref.dtype)
    out_ref[:points, slab:] = (-qsin).astype(out_ref.dtype)
    out_ref[points:, :slab] = qsin.astype(out_ref.dtype)
    out_ref[points:, slab:] = qcos.astype(out_ref.dtype)


def q_matrix(q_index, phon_vectors, degeneracy):
    points, slab = q_index.shape[1], phon_vectors.shape[1]
    return pl.pallas_call(
        q_matrix_kernel,
        out_shape=jax.ShapeDtypeStruct((2 * points, 2 * slab), jnp.bfloat16),
        compiler_params=pltpu.CompilerParams(vmem_limit_bytes=VMEM_LIMIT),
    )(q_index, phon_vectors, degeneracy.reshape(1, slab))


def bloch_kernel(places, me_ref, qmat_ref, *refs):
    count = len(places)
    slabs, out_hbm, buffers, sems = refs[:count], refs[-count - 2], refs[-count - 1 : -1], refs[-1]
    points, width = out_hbm.shape[1:]
    copies = []
    for (other, stream), slab_ref, buffer in zip(places, slabs, buffers):
        for j, chip in enumerate(CHIPS):
            result = jnp.dot(qmat_ref[...], slab_ref[j], preferred_element_type=jnp.float32).astype(buffer.dtype)
            buffer[j, 0] = result[:points]
            buffer[j, 1] = result[points:]
            place = columns_at(me_ref[0], (other, chip), stream, width)
            copies.append(pltpu.make_async_copy(buffer.at[j], out_hbm.at[:, :, place], sems.at[len(copies)]))
            copies[-1].start()
    for copy in copies:
        copy.wait()


def bloch(me, qmat, pieces, width, out=None):
    slabs = [slab for slab, _, _ in pieces]
    places = [(other, stream) for _, other, stream in pieces]
    columns = sum(slab.shape[0] * slab.shape[2] for slab in slabs)
    points = qmat.shape[0] // 2
    vmem, hbm = pl.BlockSpec(memory_space=pltpu.VMEM), pl.BlockSpec(memory_space=pltpu.HBM)
    before = () if out is None else (out,)
    return pl.pallas_call(
        lambda *refs: bloch_kernel(places, *refs),
        in_specs=[pl.BlockSpec(memory_space=pltpu.SMEM), vmem] + [vmem] * len(slabs) + [hbm] * len(before),
        out_specs=hbm,
        out_shape=jax.ShapeDtypeStruct((2, points, width), jnp.bfloat16),
        scratch_shapes=[pltpu.VMEM((slab.shape[0], 2, points, slab.shape[2]), jnp.bfloat16) for slab in slabs]
        + [pltpu.SemaphoreType.DMA((sum(slab.shape[0] for slab in slabs),))],
        input_output_aliases={2 + len(slabs): 0} if before else {},
        compiler_params=pltpu.CompilerParams(vmem_limit_bytes=VMEM_LIMIT),
        cost_estimate=pl.CostEstimate(
            flops=2 * qmat.size * columns,
            bytes_accessed=4 * points * columns,
            transcendentals=0,
        ),
    )(me, qmat, *slabs, *before)


def after(value, *others):
    return lax.optimization_barrier((value, *others))[0]


def on_device(devices, couplings, elec_vectors, phon_vectors, degeneracy, k_point, q_index):
    width = couplings.shape[3]
    wire, full = jnp.bfloat16, jnp.float32
    me = lax.axis_index("blk").astype(jnp.int32).reshape(1)
    streams = range(len(STREAMS))
    last = len(STREAMS) - 1

    def send(array, bits, name):
        with jax.named_scope(name):
            return lax.ppermute(array, "blk", [(i, i ^ bits) for i in range(devices)])

    def to_core(array, name):
        return send(array, 1, name)

    got, first, total, block = {}, {}, {}, {}
    kmat, theirs = partial_sums(me, (k_point, elec_vectors), couplings, [(1, 0, wire)])
    got[0] = to_core(theirs, "core_sum0")
    for s in streams:
        here = me if s == 0 else after(me, first[s - 1])
        pieces = [(0, s, full)] + [(1, s + 1, wire)] * (s < last)
        own, *theirs = partial_sums(here, kmat, couplings, pieces)
        if theirs:
            got[s + 1] = to_core(theirs[0], f"core_sum{s + 1}")
        total[s] = own + got[s].astype(full)
        parts = [total[s][i : i + 1].astype(wire) for i in SUM_ORDER]
        first[s] = parts[0]
        got[s] = [send(part, SQUARE[i], f"square_sum{s}") for i, part in zip(SUM_ORDER, parts)]
    for s in streams:
        own = total[s][3:]
        if s == last:
            qmat = q_matrix(after(q_index, early), phon_vectors, degeneracy)
            own = after(own, qmat)
        for array in got[s]:
            own = own + array.astype(full)
        early = own.astype(wire)
        step = 8
        while step < devices:
            own = own + send(own.astype(wire), step + 4 * MIRROR[s] * (step == 8), f"far_sum{s}").astype(full)
            step *= 2
        block[s] = own.astype(wire)

    for s in streams:
        back = {i: send(block[s], SQUARE[i], f"square_gather{s}") for i in GATHER_ORDER}
        got[s] = [back[i] for i in range(3)]

    out = None
    for s in streams:
        if s:
            got[s][0] = after(got[s][0], out)
        mine = jnp.concatenate([*got[s], block[s]])
        pieces = [(mine, 0, s)] if s == 0 else [(theirs, 1, s - 1), (mine, 0, s)]
        theirs = to_core(mine, f"core_gather{s}")
        out = bloch(me, qmat, pieces, width, out)
    return bloch(me, qmat, [(theirs, 1, last)], width, out)


def solution(mesh):
    placed = (
        P("blk", None, "grp", None),
        P(None, "blk"),
        P(None, "grp"),
        P("grp"),
        P("grp"),
        P(None, "blk"),
    )
    devices = mesh.shape["blk"]
    return jax.shard_map(
        lambda *arrays: on_device(devices, *arrays),
        mesh=mesh,
        in_specs=placed,
        out_specs=P(None, ("grp", "blk"), None),
        check_vma=False,
    )
```

```python
import math

import jax
import jax.numpy as jnp
from jax import lax
from jax.experimental import pallas as pl
from jax.experimental.pallas import tpu as pltpu
from jax.sharding import PartitionSpec as P

NG = 16
STREAMS = (1, 1)
BLOCKS = 8
SHARE = (1, 4)
LANES = 128
VMEM_LIMIT = 24 * 2**20

CHIPS = ("across", "x", "z", "own")
SQUARE = (6, 2, 4)
SUM_ORDER = (2, 0, 1)
GATHER_ORDER = (2, 0, 1)
MIRROR = (0, 1)


def block_of(me, place, stream):
    other, chip = place
    core, x, z = me % 2, (me // 2) % 2, (me // 4 + MIRROR[stream] * (me // 8)) % 2
    flip_x, flip_z = {"across": (1, 1), "x": (1, 0), "z": (0, 1), "own": (0, 0)}[chip]
    return (core + other) % 2 * 4 + (x + flip_x) % 2 * 2 + (z + flip_z) % 2


def stream_columns(width, stream):
    unit = width // BLOCKS // sum(STREAMS)
    return sum(STREAMS[:stream]) * unit * BLOCKS, STREAMS[stream] * unit


def columns_at(me, place, stream, width):
    start, columns = stream_columns(width, stream)
    start = start + block_of(me, place, stream) * columns
    return pl.ds(pl.multiple_of(start, 128), columns)


def phase_matrix(k_row, elec_vectors, shape, slab, parts):
    rows, depth = shape
    terms = [k_row[:, d : d + 1] * elec_vectors[d : d + 1, :].astype(jnp.float32) for d in range(3)]
    theta_here = 2.0 * math.pi * (terms[0] + terms[1] + terms[2])
    vector = lax.broadcasted_iota(jnp.int32, (8, depth), 1) // (parts * slab)
    theta = jnp.zeros((8, depth), jnp.float32)
    for e in range(elec_vectors.shape[1]):
        theta = jnp.where(vector == e, theta_here[:, e : e + 1], theta)
    cos = jnp.cos(theta)[:1]
    sin = jnp.sin(theta)[:1]
    row = lax.broadcasted_iota(jnp.int32, shape, 0)
    col = lax.broadcasted_iota(jnp.int32, shape, 1)
    out_part, in_part = row // slab, (col // slab) % parts
    value = jnp.where(out_part == in_part, cos, jnp.where(out_part == 1, sin, -sin))
    return jnp.where(row % slab == col % slab, value, 0.0).astype(jnp.bfloat16)


def partial_kernel(pieces, given, me_ref, *refs):
    *refs, sems = refs
    refs, tables = refs[: -len(pieces)], refs[-len(pieces) :]
    if given:
        kmat_in, couplings_hbm, *outs = refs
    else:
        k_hbm, elec_hbm, couplings_hbm, kmat_out, *outs, k_buf, elec_buf, small = refs
        small_copies = [
            pltpu.make_async_copy(k_hbm, k_buf, small.at[0]),
            pltpu.make_async_copy(elec_hbm, elec_buf, small.at[1]),
        ]
        for copy in small_copies:
            copy.start()
    re_here, parts, slab = couplings_hbm.shape[:3]
    rows, depth = parts * slab, re_here * parts * slab
    width = couplings_hbm.shape[3]
    copies = []
    for piece, (other, stream, _) in enumerate(pieces):
        for j, chip in enumerate(CHIPS):
            place = columns_at(me_ref[0], (other, chip), stream, width)
            n = len(copies)
            copies.append(pltpu.make_async_copy(couplings_hbm.at[:, :, :, place], tables[piece].at[j], sems.at[n]))
            copies[-1].start()
    if given:
        kmat = kmat_in[...]
    else:
        for copy in small_copies:
            copy.wait()
        kmat = phase_matrix(k_buf[...], elec_buf[...], (rows, depth), slab, parts)
        kmat_out[...] = kmat
    here = [
        tuple(kmat[r : r + 1, e * rows : e * rows + 1].astype(jnp.float32) for r in (0, slab)) for e in range(re_here)
    ]
    for n, copy in enumerate(copies):
        out_ref, table = outs[n // len(CHIPS)], tables[n // len(CHIPS)]
        columns = out_ref.shape[-1]
        split = columns * SHARE[0] // SHARE[1] // 128 * 128 if given else 0
        copy.wait()
        if split:
            flat = table[n % len(CHIPS), :, :, :, :split].reshape(depth, split)
            out_ref[n % len(CHIPS), :, :split] = jnp.dot(kmat, flat, preferred_element_type=jnp.float32).astype(out_ref.dtype)
        for low in range(split, columns, LANES):
            place = pl.ds(low, min(LANES, columns - low))
            real = imag = 0.0
            for e, (cos, sin) in enumerate(here):
                a = table[n % len(CHIPS), e, 0, :, place].astype(jnp.float32)
                b = table[n % len(CHIPS), e, 1, :, place].astype(jnp.float32)
                real, imag = real + (cos * a - sin * b), imag + (sin * a + cos * b)
            out_ref[n % len(CHIPS), :slab, place] = real.astype(out_ref.dtype)
            out_ref[n % len(CHIPS), slab:, place] = imag.astype(out_ref.dtype)


def partial_sums(me, phases, couplings, pieces):
    re_here, parts, slab, width = couplings.shape
    sizes = [stream_columns(width, stream)[1] for _, stream, _ in pieces]
    rows, depth = parts * slab, re_here * parts * slab
    hbm, vmem = pl.BlockSpec(memory_space=pltpu.HBM), pl.BlockSpec(memory_space=pltpu.VMEM)
    given = not isinstance(phases, tuple)
    if given:
        operands, specs, first_out, small = [phases], [vmem], [], []
    else:
        k_point, elec_vectors = phases
        operands = [pltpu.with_memory_space_constraint(a, pltpu.HBM) for a in (k_point.reshape(1, 3), elec_vectors)]
        specs, first_out = [hbm, hbm], [jax.ShapeDtypeStruct((rows, depth), jnp.bfloat16)]
        small = [
            pltpu.VMEM((1, 3), jnp.float32),
            pltpu.VMEM(elec_vectors.shape, jnp.int32),
            pltpu.SemaphoreType.DMA((2,)),
        ]
    copies = len(CHIPS) * len(pieces)
    outs = first_out + [jax.ShapeDtypeStruct((len(CHIPS), rows, n), dtype) for (_, _, dtype), n in zip(pieces, sizes)]
    return pl.pallas_call(
        lambda *refs: partial_kernel(pieces, given, *refs),
        in_specs=[pl.BlockSpec(memory_space=pltpu.SMEM), *specs, hbm],
        out_specs=[vmem] * len(outs),
        out_shape=outs,
        scratch_shapes=small
        + [pltpu.VMEM((len(CHIPS), re_here, parts, slab, n), couplings.dtype) for n in sizes]
        + [pltpu.SemaphoreType.DMA((copies,))],
        compiler_params=pltpu.CompilerParams(vmem_limit_bytes=VMEM_LIMIT),
        cost_estimate=pl.CostEstimate(
            flops=2 * rows * depth * len(CHIPS) * sum(sizes),
            bytes_accessed=2 * depth * len(CHIPS) * sum(sizes),
            transcendentals=0,
        ),
    )(me, *operands, pltpu.with_memory_space_constraint(couplings, pltpu.HBM))


def q_matrix_kernel(q_ref, phon_ref, degeneracy_ref, out_ref):
    points, slab = out_ref.shape[0] // 2, out_ref.shape[1] // 2
    dots = lax.dot_general(
        q_ref[...].astype(jnp.float32),
        phon_ref[...].astype(jnp.float32),
        (((0,), (0,)), ((), ())),
        preferred_element_type=jnp.float32,
    )
    wound = jnp.bitwise_and(dots.astype(jnp.int32), NG - 1).astype(jnp.float32)
    angle = 2.0 * math.pi * wound / NG
    weight = 1.0 / degeneracy_ref[...].astype(jnp.float32)
    qcos = jnp.cos(angle) * weight
    qsin = jnp.sin(angle) * weight
    out_ref[:points, :slab] = qcos.astype(out_ref.dtype)
    out_ref[:points, slab:] = (-qsin).astype(out_ref.dtype)
    out_ref[points:, :slab] = qsin.astype(out_ref.dtype)
    out_ref[points:, slab:] = qcos.astype(out_ref.dtype)


def q_matrix(q_index, phon_vectors, degeneracy):
    points, slab = q_index.shape[1], phon_vectors.shape[1]
    return pl.pallas_call(
        q_matrix_kernel,
        out_shape=jax.ShapeDtypeStruct((2 * points, 2 * slab), jnp.bfloat16),
        compiler_params=pltpu.CompilerParams(vmem_limit_bytes=VMEM_LIMIT),
    )(q_index, phon_vectors, degeneracy.reshape(1, slab))


def bloch_kernel(places, me_ref, qmat_ref, *refs):
    count = len(places)
    slabs, out_hbm, buffers, sems = refs[:count], refs[-count - 2], refs[-count - 1 : -1], refs[-1]
    points, width = out_hbm.shape[1:]
    copies = []
    for (other, stream), slab_ref, buffer in zip(places, slabs, buffers):
        for j, chip in enumerate(CHIPS):
            result = jnp.dot(qmat_ref[...], slab_ref[j], preferred_element_type=jnp.float32).astype(buffer.dtype)
            buffer[j, 0] = result[:points]
            buffer[j, 1] = result[points:]
            place = columns_at(me_ref[0], (other, chip), stream, width)
            copies.append(pltpu.make_async_copy(buffer.at[j], out_hbm.at[:, :, place], sems.at[len(copies)]))
            copies[-1].start()
    for copy in copies:
        copy.wait()


def bloch(me, qmat, pieces, width, out=None):
    slabs = [slab for slab, _, _ in pieces]
    places = [(other, stream) for _, other, stream in pieces]
    columns = sum(slab.shape[0] * slab.shape[2] for slab in slabs)
    points = qmat.shape[0] // 2
    vmem, hbm = pl.BlockSpec(memory_space=pltpu.VMEM), pl.BlockSpec(memory_space=pltpu.HBM)
    before = () if out is None else (out,)
    return pl.pallas_call(
        lambda *refs: bloch_kernel(places, *refs),
        in_specs=[pl.BlockSpec(memory_space=pltpu.SMEM), vmem] + [vmem] * len(slabs) + [hbm] * len(before),
        out_specs=hbm,
        out_shape=jax.ShapeDtypeStruct((2, points, width), jnp.bfloat16),
        scratch_shapes=[pltpu.VMEM((slab.shape[0], 2, points, slab.shape[2]), jnp.bfloat16) for slab in slabs]
        + [pltpu.SemaphoreType.DMA((sum(slab.shape[0] for slab in slabs),))],
        input_output_aliases={2 + len(slabs): 0} if before else {},
        compiler_params=pltpu.CompilerParams(vmem_limit_bytes=VMEM_LIMIT),
        cost_estimate=pl.CostEstimate(
            flops=2 * qmat.size * columns,
            bytes_accessed=4 * points * columns,
            transcendentals=0,
        ),
    )(me, qmat, *slabs, *before)


def after(value, *others):
    return lax.optimization_barrier((value, *others))[0]


def on_device(devices, couplings, elec_vectors, phon_vectors, degeneracy, k_point, q_index):
    width = couplings.shape[3]
    wire, full = jnp.bfloat16, jnp.float32
    me = lax.axis_index("blk").astype(jnp.int32).reshape(1)
    streams = range(len(STREAMS))
    last = len(STREAMS) - 1

    def send(array, bits, name):
        with jax.named_scope(name):
            return lax.ppermute(array, "blk", [(i, i ^ bits) for i in range(devices)])

    def to_core(array, name):
        return send(array, 1, name)

    got, first, total, block = {}, {}, {}, {}
    kmat, theirs = partial_sums(me, (k_point, elec_vectors), couplings, [(1, 0, wire)])
    got[0] = to_core(theirs, "core_sum0")
    for s in streams:
        here = me if s == 0 else after(me, first[s - 1])
        pieces = [(0, s, full)] + [(1, s + 1, wire)] * (s < last)
        own, *theirs = partial_sums(here, kmat, couplings, pieces)
        total[s] = own + got[s].astype(full)
        parts = [total[s][i : i + 1].astype(wire) for i in SUM_ORDER]
        first[s] = parts[0]
        got[s] = [send(part, SQUARE[i], f"square_sum{s}") for i, part in zip(SUM_ORDER, parts)]
        if theirs:
            got[s + 1] = to_core(after(theirs[0], parts[0]), f"core_sum{s + 1}")
    for s in streams:
        own = total[s][3:]
        if s == last:
            qmat = q_matrix(after(q_index, early), phon_vectors, degeneracy)
            own = after(own, qmat)
        for array in got[s]:
            own = own + array.astype(full)
        early = own.astype(wire)
        step = 8
        while step < devices:
            own = own + send(own.astype(wire), step + 4 * MIRROR[s] * (step == 8), f"far_sum{s}").astype(full)
            step *= 2
        block[s] = own.astype(wire)

    for s in streams:
        back = {i: send(block[s], SQUARE[i], f"square_gather{s}") for i in GATHER_ORDER}
        got[s] = [back[i] for i in range(3)]

    out = None
    for s in streams:
        if s:
            got[s][0] = after(got[s][0], out)
        mine = jnp.concatenate([*got[s], block[s]])
        pieces = [(mine, 0, s)] if s == 0 else [(theirs, 1, s - 1), (mine, 0, s)]
        theirs = to_core(mine, f"core_gather{s}")
        out = bloch(me, qmat, pieces, width, out)
    return bloch(me, qmat, [(theirs, 1, last)], width, out)


def solution(mesh):
    placed = (
        P("blk", None, "grp", None),
        P(None, "blk"),
        P(None, "grp"),
        P("grp"),
        P("grp"),
        P(None, "blk"),
    )
    devices = mesh.shape["blk"]
    return jax.shard_map(
        lambda *arrays: on_device(devices, *arrays),
        mesh=mesh,
        in_specs=placed,
        out_specs=P(None, ("grp", "blk"), None),
        check_vma=False,
    )
```

```python
import math

import jax
import jax.numpy as jnp
from jax import lax
from jax.experimental import pallas as pl
from jax.experimental.pallas import tpu as pltpu
from jax.sharding import PartitionSpec as P

NG = 16
STREAMS = (1, 1)
BLOCKS = 8
SHARE = (1, 4)
LANES = 128
VMEM_LIMIT = 24 * 2**20

CHIPS = ("across", "x", "z", "own")
SQUARE = (6, 2, 4)
SUM_ORDER = (2, 0, 1)
GATHER_ORDERS = ((2, 0, 1), (0, 2, 1))
MIRROR = (0, 1)


def block_of(me, place, stream):
    other, chip = place
    core, x, z = me % 2, (me // 2) % 2, (me // 4 + MIRROR[stream] * (me // 8)) % 2
    flip_x, flip_z = {"across": (1, 1), "x": (1, 0), "z": (0, 1), "own": (0, 0)}[chip]
    return (core + other) % 2 * 4 + (x + flip_x) % 2 * 2 + (z + flip_z) % 2


def stream_columns(width, stream):
    unit = width // BLOCKS // sum(STREAMS)
    return sum(STREAMS[:stream]) * unit * BLOCKS, STREAMS[stream] * unit


def columns_at(me, place, stream, width):
    start, columns = stream_columns(width, stream)
    start = start + block_of(me, place, stream) * columns
    return pl.ds(pl.multiple_of(start, 128), columns)


def phase_matrix(k_row, elec_vectors, shape, slab, parts):
    rows, depth = shape
    terms = [k_row[:, d : d + 1] * elec_vectors[d : d + 1, :].astype(jnp.float32) for d in range(3)]
    theta_here = 2.0 * math.pi * (terms[0] + terms[1] + terms[2])
    vector = lax.broadcasted_iota(jnp.int32, (8, depth), 1) // (parts * slab)
    theta = jnp.zeros((8, depth), jnp.float32)
    for e in range(elec_vectors.shape[1]):
        theta = jnp.where(vector == e, theta_here[:, e : e + 1], theta)
    cos = jnp.cos(theta)[:1]
    sin = jnp.sin(theta)[:1]
    row = lax.broadcasted_iota(jnp.int32, shape, 0)
    col = lax.broadcasted_iota(jnp.int32, shape, 1)
    out_part, in_part = row // slab, (col // slab) % parts
    value = jnp.where(out_part == in_part, cos, jnp.where(out_part == 1, sin, -sin))
    return jnp.where(row % slab == col % slab, value, 0.0).astype(jnp.bfloat16)


def partial_kernel(pieces, given, me_ref, *refs):
    *refs, sems = refs
    refs, tables = refs[: -len(pieces)], refs[-len(pieces) :]
    if given:
        kmat_in, couplings_hbm, *outs = refs
    else:
        k_hbm, elec_hbm, couplings_hbm, kmat_out, *outs, k_buf, elec_buf, small = refs
        small_copies = [
            pltpu.make_async_copy(k_hbm, k_buf, small.at[0]),
            pltpu.make_async_copy(elec_hbm, elec_buf, small.at[1]),
        ]
        for copy in small_copies:
            copy.start()
    re_here, parts, slab = couplings_hbm.shape[:3]
    rows, depth = parts * slab, re_here * parts * slab
    width = couplings_hbm.shape[3]
    copies = []
    for piece, (other, stream, _) in enumerate(pieces):
        for j, chip in enumerate(CHIPS):
            place = columns_at(me_ref[0], (other, chip), stream, width)
            n = len(copies)
            copies.append(pltpu.make_async_copy(couplings_hbm.at[:, :, :, place], tables[piece].at[j], sems.at[n]))
            copies[-1].start()
    if given:
        kmat = kmat_in[...]
    else:
        for copy in small_copies:
            copy.wait()
        kmat = phase_matrix(k_buf[...], elec_buf[...], (rows, depth), slab, parts)
        kmat_out[...] = kmat
    here = [
        tuple(kmat[r : r + 1, e * rows : e * rows + 1].astype(jnp.float32) for r in (0, slab)) for e in range(re_here)
    ]
    for n, copy in enumerate(copies):
        out_ref, table = outs[n // len(CHIPS)], tables[n // len(CHIPS)]
        columns = out_ref.shape[-1]
        split = columns * SHARE[0] // SHARE[1] // 128 * 128
        copy.wait()
        if split:
            flat = table[n % len(CHIPS), :, :, :, :split].reshape(depth, split)
            out_ref[n % len(CHIPS), :, :split] = jnp.dot(kmat, flat, preferred_element_type=jnp.float32).astype(out_ref.dtype)
        for low in range(split, columns, LANES):
            place = pl.ds(low, min(LANES, columns - low))
            real = imag = 0.0
            for e, (cos, sin) in enumerate(here):
                a = table[n % len(CHIPS), e, 0, :, place].astype(jnp.float32)
                b = table[n % len(CHIPS), e, 1, :, place].astype(jnp.float32)
                real, imag = real + (cos * a - sin * b), imag + (sin * a + cos * b)
            out_ref[n % len(CHIPS), :slab, place] = real.astype(out_ref.dtype)
            out_ref[n % len(CHIPS), slab:, place] = imag.astype(out_ref.dtype)


def partial_sums(me, phases, couplings, pieces):
    re_here, parts, slab, width = couplings.shape
    sizes = [stream_columns(width, stream)[1] for _, stream, _ in pieces]
    rows, depth = parts * slab, re_here * parts * slab
    hbm, vmem = pl.BlockSpec(memory_space=pltpu.HBM), pl.BlockSpec(memory_space=pltpu.VMEM)
    given = not isinstance(phases, tuple)
    if given:
        operands, specs, first_out, small = [phases], [vmem], [], []
    else:
        k_point, elec_vectors = phases
        operands = [pltpu.with_memory_space_constraint(a, pltpu.HBM) for a in (k_point.reshape(1, 3), elec_vectors)]
        specs, first_out = [hbm, hbm], [jax.ShapeDtypeStruct((rows, depth), jnp.bfloat16)]
        small = [
            pltpu.VMEM((1, 3), jnp.float32),
            pltpu.VMEM(elec_vectors.shape, jnp.int32),
            pltpu.SemaphoreType.DMA((2,)),
        ]
    copies = len(CHIPS) * len(pieces)
    outs = first_out + [jax.ShapeDtypeStruct((len(CHIPS), rows, n), dtype) for (_, _, dtype), n in zip(pieces, sizes)]
    return pl.pallas_call(
        lambda *refs: partial_kernel(pieces, given, *refs),
        in_specs=[pl.BlockSpec(memory_space=pltpu.SMEM), *specs, hbm],
        out_specs=[vmem] * len(outs),
        out_shape=outs,
        scratch_shapes=small
        + [pltpu.VMEM((len(CHIPS), re_here, parts, slab, n), couplings.dtype) for n in sizes]
        + [pltpu.SemaphoreType.DMA((copies,))],
        compiler_params=pltpu.CompilerParams(vmem_limit_bytes=VMEM_LIMIT),
        cost_estimate=pl.CostEstimate(
            flops=2 * rows * depth * len(CHIPS) * sum(sizes),
            bytes_accessed=2 * depth * len(CHIPS) * sum(sizes),
            transcendentals=0,
        ),
    )(me, *operands, pltpu.with_memory_space_constraint(couplings, pltpu.HBM))


def q_matrix_kernel(q_ref, phon_ref, degeneracy_ref, out_ref):
    points, slab = out_ref.shape[0] // 2, out_ref.shape[1] // 2
    dots = lax.dot_general(
        q_ref[...].astype(jnp.float32),
        phon_ref[...].astype(jnp.float32),
        (((0,), (0,)), ((), ())),
        preferred_element_type=jnp.float32,
    )
    wound = jnp.bitwise_and(dots.astype(jnp.int32), NG - 1).astype(jnp.float32)
    angle = 2.0 * math.pi * wound / NG
    weight = 1.0 / degeneracy_ref[...].astype(jnp.float32)
    qcos = jnp.cos(angle) * weight
    qsin = jnp.sin(angle) * weight
    out_ref[:points, :slab] = qcos.astype(out_ref.dtype)
    out_ref[:points, slab:] = (-qsin).astype(out_ref.dtype)
    out_ref[points:, :slab] = qsin.astype(out_ref.dtype)
    out_ref[points:, slab:] = qcos.astype(out_ref.dtype)


def q_matrix(q_index, phon_vectors, degeneracy):
    points, slab = q_index.shape[1], phon_vectors.shape[1]
    return pl.pallas_call(
        q_matrix_kernel,
        out_shape=jax.ShapeDtypeStruct((2 * points, 2 * slab), jnp.bfloat16),
        compiler_params=pltpu.CompilerParams(vmem_limit_bytes=VMEM_LIMIT),
    )(q_index, phon_vectors, degeneracy.reshape(1, slab))


def bloch_kernel(places, me_ref, qmat_ref, *refs):
    count = len(places)
    slabs, out_hbm, buffers, sems = refs[:count], refs[-count - 2], refs[-count - 1 : -1], refs[-1]
    points, width = out_hbm.shape[1:]
    copies = []
    for (other, stream), slab_ref, buffer in zip(places, slabs, buffers):
        for j, chip in enumerate(CHIPS):
            result = jnp.dot(qmat_ref[...], slab_ref[j], preferred_element_type=jnp.float32).astype(buffer.dtype)
            buffer[j, 0] = result[:points]
            buffer[j, 1] = result[points:]
            place = columns_at(me_ref[0], (other, chip), stream, width)
            copies.append(pltpu.make_async_copy(buffer.at[j], out_hbm.at[:, :, place], sems.at[len(copies)]))
            copies[-1].start()
    for copy in copies:
        copy.wait()


def bloch(me, qmat, pieces, width, out=None):
    slabs = [slab for slab, _, _ in pieces]
    places = [(other, stream) for _, other, stream in pieces]
    columns = sum(slab.shape[0] * slab.shape[2] for slab in slabs)
    points = qmat.shape[0] // 2
    vmem, hbm = pl.BlockSpec(memory_space=pltpu.VMEM), pl.BlockSpec(memory_space=pltpu.HBM)
    before = () if out is None else (out,)
    return pl.pallas_call(
        lambda *refs: bloch_kernel(places, *refs),
        in_specs=[pl.BlockSpec(memory_space=pltpu.SMEM), vmem] + [vmem] * len(slabs) + [hbm] * len(before),
        out_specs=hbm,
        out_shape=jax.ShapeDtypeStruct((2, points, width), jnp.bfloat16),
        scratch_shapes=[pltpu.VMEM((slab.shape[0], 2, points, slab.shape[2]), jnp.bfloat16) for slab in slabs]
        + [pltpu.SemaphoreType.DMA((sum(slab.shape[0] for slab in slabs),))],
        input_output_aliases={2 + len(slabs): 0} if before else {},
        compiler_params=pltpu.CompilerParams(vmem_limit_bytes=VMEM_LIMIT),
        cost_estimate=pl.CostEstimate(
            flops=2 * qmat.size * columns,
            bytes_accessed=4 * points * columns,
            transcendentals=0,
        ),
    )(me, qmat, *slabs, *before)


def after(value, *others):
    return lax.optimization_barrier((value, *others))[0]


def on_device(devices, couplings, elec_vectors, phon_vectors, degeneracy, k_point, q_index):
    width = couplings.shape[3]
    wire, full = jnp.bfloat16, jnp.float32
    me = lax.axis_index("blk").astype(jnp.int32).reshape(1)
    streams = range(len(STREAMS))
    last = len(STREAMS) - 1

    def send(array, bits, name):
        with jax.named_scope(name):
            return lax.ppermute(array, "blk", [(i, i ^ bits) for i in range(devices)])

    def to_core(array, name):
        return send(array, 1, name)

    got, first, total, block = {}, {}, {}, {}
    kmat, theirs = partial_sums(me, (k_point, elec_vectors), couplings, [(1, 0, wire)])
    got[0] = to_core(theirs, "core_sum0")
    for s in streams:
        here = me if s == 0 else after(me, first[s - 1])
        pieces = [(0, s, full)] + [(1, s + 1, wire)] * (s < last)
        own, *theirs = partial_sums(here, kmat, couplings, pieces)
        if theirs:
            got[s + 1] = to_core(theirs[0], f"core_sum{s + 1}")
        total[s] = own + got[s].astype(full)
        parts = [total[s][i : i + 1].astype(wire) for i in SUM_ORDER]
        first[s] = parts[0]
        got[s] = [send(part, SQUARE[i], f"square_sum{s}") for i, part in zip(SUM_ORDER, parts)]
    for s in streams:
        own = total[s][3:]
        if s == last:
            qmat = q_matrix(after(q_index, early), phon_vectors, degeneracy)
            own = after(own, qmat)
        for array in got[s]:
            own = own + array.astype(full)
        early = own.astype(wire)
        step = 8
        while step < devices:
            own = own + send(own.astype(wire), step + 4 * MIRROR[s] * (step == 8), f"far_sum{s}").astype(full)
            step *= 2
        block[s] = own.astype(wire)

    for s in streams:
        back = {i: send(block[s], SQUARE[i], f"square_gather{s}") for i in GATHER_ORDERS[s]}
        got[s] = [back[i] for i in range(3)]

    out = None
    for s in streams:
        if s:
            got[s][0] = after(got[s][0], out)
        mine = jnp.concatenate([*got[s], block[s]])
        pieces = [(mine, 0, s)] if s == 0 else [(theirs, 1, s - 1), (mine, 0, s)]
        theirs = to_core(mine, f"core_gather{s}")
        out = bloch(me, qmat, pieces, width, out)
    return bloch(me, qmat, [(theirs, 1, last)], width, out)


def solution(mesh):
    placed = (
        P("blk", None, "grp", None),
        P(None, "blk"),
        P(None, "grp"),
        P("grp"),
        P("grp"),
        P(None, "blk"),
    )
    devices = mesh.shape["blk"]
    return jax.shard_map(
        lambda *arrays: on_device(devices, *arrays),
        mesh=mesh,
        in_specs=placed,
        out_specs=P(None, ("grp", "blk"), None),
        check_vma=False,
    )
```
